32 devices in a mesh: wide: 16 (over z, y, x), narrow: 2 (over core).
Axes of the slice: x: 2, y: 2, z: 4, core: 2. Of those that a mesh axis runs over, the one named last changes fastest.
Arguments:
- amplitudes: bfloat16 [256, 256, 128], P('wide', 'narrow'), may hold values from -6 to 6
- send_list: int32 [16, 32], P('wide'), may hold values from 0 to 15
- tile_positions: int32 [128, 16], P('wide', 'narrow'), may hold values from 0 to 31
- integrals: bfloat16 [128, 16, 128, 128], P('wide', 'narrow'), may hold values from -0.125 to 0.125
Outputs:
- ladder: bfloat16 [128, 256, 128], P('wide', 'narrow')
The draws below stay inside these ranges and needn't reach their ends.
All inputs are finite; a program needn't handle non-finite values.
Results may differ from the reference program's by a relative error of at most 0.001.
Values may be sent and summed in bfloat16 or wider, within the bound.
No kernel may reach another device: no remote copies, remote signals or barrier semaphores. Data moves between devices by JAX's collectives and lax.ppermute only.
A program may use at most 64 MiB of HBM per device.

```python
import jax
import jax.numpy as jnp
from jax import lax

TILE = 128
XT_DEV = 8
AMP_DEV = 16
KI = 16
CAP = 2
PAIRS = 256
NX = 128
NY = 256
N_WIDE = 16


def touch_ends(drawn, own_key, smallest, top_value):
    longest = drawn.shape.index(max(drawn.shape))
    spots = []
    for shift in (0, 1):
        where = [jax.random.randint(jax.random.fold_in(own_key, axis), (), 0, length) for axis, length in enumerate(drawn.shape)]
        where[longest] = (where[longest] + shift) % drawn.shape[longest]
        spots.append(tuple(where))
    return drawn.at[spots[0]].set(smallest).at[spots[1]].set(top_value)


def level_of(key, dims, cuts, smallest, top_value):
    level = 1.0
    for dim, blocks in cuts:
        draws = jax.random.uniform(jax.random.fold_in(jax.random.fold_in(key, 6), dim), (blocks,), jnp.float32, smallest / len(cuts), top_value / len(cuts))
        level = level * jnp.repeat(jnp.exp(draws), dims[dim] // blocks).reshape((-1,) + (1,) * (len(dims) - 1 - dim))
    return level


def bell_draw(key, dims, deviation, reach, pieces=(), kind=jnp.bfloat16):
    values = deviation * jax.random.normal(key, dims, jnp.float32)
    if pieces:
        values = values * level_of(key, dims, pieces, -0.22, 0.18)
    return jnp.clip(values, -reach, reach).astype(kind)


def setup_inputs(seed: int = 0) -> dict:
    keys = jax.random.split(jax.random.key(seed), 5)
    amplitudes = bell_draw(keys[0], (NY, PAIRS, TILE), 1.0, 6.0, ((0, 16), (1, 2)))
    send_list = touch_ends(jax.random.randint(keys[1], (N_WIDE, N_WIDE * CAP), 0, AMP_DEV), jax.random.fold_in(keys[1], 1), 0, AMP_DEV - 1).astype(jnp.int32)
    tile_positions = touch_ends(jax.random.randint(keys[2], (NX, KI), 0, N_WIDE * CAP), jax.random.fold_in(keys[2], 1), 0, (N_WIDE * CAP) - 1).astype(jnp.int32)
    integrals = bell_draw(keys[3], (NX, KI, TILE, TILE), (KI * TILE) ** -0.5, 0.125, ((0, 16), (1, 2)))
    return dict(amplitudes=amplitudes, send_list=send_list, tile_positions=tile_positions, integrals=integrals)


def reference(amplitudes, send_list, tile_positions, integrals):
    rows = jnp.arange(NX, dtype=jnp.int32)[:, None]
    device = rows // XT_DEV
    owner = tile_positions // CAP
    slot = tile_positions % CAP
    source = owner * AMP_DEV + send_list[owner, device * CAP + slot]

    def one_tile(args):
        picks, blocks = args
        tiles = amplitudes[picks]
        flat = jnp.transpose(tiles, (1, 0, 2)).reshape(PAIRS, KI * TILE)
        return jnp.dot(flat, blocks.reshape(KI * TILE, TILE), preferred_element_type=jnp.float32).astype(jnp.bfloat16)

    return lax.map(one_tile, (source.astype(jnp.int32), integrals))
```

```python
import functools

import jax
import jax.numpy as jnp
from jax import lax
from jax.experimental import pallas as pl
from jax.experimental.pallas import tpu as pltpu
from jax.sharding import PartitionSpec as P

VMEM_LIMIT = 48 * 1024 * 1024


def pick_outgoing(send_ref, amplitudes_ref, out_ref):
    for slot in range(out_ref.shape[0]):
        out_ref[slot] = amplitudes_ref[send_ref[0, slot]]


def contract(half_count, *refs):
    places = refs[:half_count]
    received_ref = refs[half_count]
    blocks = refs[half_count + 1 : 2 * half_count + 1]
    out_ref, stage, sems = refs[2 * half_count + 1 :]
    tiles, per_half, inner, columns = blocks[0].shape
    copies = []
    for x in range(tiles):
        total = None
        for place_ref, block_ref in zip(places, blocks):
            picked = jnp.concatenate(
                [received_ref[place_ref[x, k]] for k in range(per_half)], axis=1
            )
            part = jnp.dot(
                picked,
                block_ref[x].reshape(per_half * inner, columns),
                preferred_element_type=jnp.float32,
            )
            total = part if total is None else total + part
        stage[x] = total.astype(stage.dtype)
        copy = pltpu.make_async_copy(stage.at[x], out_ref.at[x], sems.at[x])
        copy.start()
        copies.append(copy)
    for copy in copies:
        copy.wait()


def on_device(narrow, amplitudes, send_list, tile_positions, integrals):
    smem = pl.BlockSpec(memory_space=pltpu.SMEM)
    vmem = pl.BlockSpec(memory_space=pltpu.VMEM)
    params = pltpu.CompilerParams(vmem_limit_bytes=VMEM_LIMIT)
    slots = send_list.shape[1]
    tile_bytes = amplitudes.shape[1] * amplitudes.shape[2] * 2
    outgoing = pl.pallas_call(
        pick_outgoing,
        out_shape=jax.ShapeDtypeStruct((slots,) + amplitudes.shape[1:], amplitudes.dtype),
        in_specs=[smem, vmem],
        out_specs=vmem,
        compiler_params=params,
        cost_estimate=pl.CostEstimate(flops=0, bytes_accessed=2 * slots * tile_bytes, transcendentals=0),
    )(send_list, amplitudes)
    if narrow == 2:
        swap = [(0, 1), (1, 0)]
        places = [tile_positions, lax.ppermute(tile_positions, "narrow", swap)]
        blocks = [integrals, lax.ppermute(integrals, "narrow", swap)]
    else:
        places = [lax.all_gather(tile_positions, "narrow", axis=1, tiled=True)]
        blocks = [lax.all_gather(integrals, "narrow", axis=1, tiled=True)]
    received = lax.all_to_all(outgoing, "wide", split_axis=0, concat_axis=0, tiled=True)
    tiles, pairs, columns = integrals.shape[0], amplitudes.shape[1], integrals.shape[3]
    count = len(blocks)
    return pl.pallas_call(
        functools.partial(contract, count),
        out_shape=jax.ShapeDtypeStruct((tiles, pairs, columns), jnp.bfloat16),
        in_specs=[smem] * count + [vmem] * (count + 1),
        out_specs=pl.BlockSpec(memory_space=pl.ANY),
        scratch_shapes=[
            pltpu.VMEM((tiles, pairs, columns), jnp.bfloat16),
            pltpu.SemaphoreType.DMA((tiles,)),
        ],
        compiler_params=params,
    )(*places, received, *blocks)


def solution(mesh):
    placed = (
        P("wide", "narrow", None),
        P("wide", None),
        P("wide", "narrow"),
        P("wide", "narrow", None, None),
    )
    return jax.shard_map(
        functools.partial(on_device, mesh.shape["narrow"]),
        mesh=mesh,
        in_specs=placed,
        out_specs=P("wide", "narrow", None),
        check_vma=False,
    )
```

```python
import functools

import jax
import jax.numpy as jnp
from jax import lax
from jax.experimental import pallas as pl
from jax.experimental.pallas import tpu as pltpu
from jax.sharding import PartitionSpec as P

VMEM_LIMIT = 48 * 1024 * 1024
DIRECT_WIDE = 16


def pick_outgoing(partners, send_ref, amplitudes_ref, *refs):
    out_refs = refs[: len(partners)]
    sends, held, sems = refs[len(partners) :]
    fetch_sends = pltpu.make_async_copy(send_ref, sends, sems.at[0])
    fetch_tiles = pltpu.make_async_copy(amplitudes_ref, held, sems.at[1])
    fetch_sends.start()
    fetch_tiles.start()
    fetch_sends.wait()
    fetch_tiles.wait()
    me = lax.axis_index("wide")
    for partner, out_ref in zip(partners, out_refs):
        cap = out_ref.shape[0]
        for slot in range(cap):
            out_ref[slot] = held[sends[0, (me ^ partner) * cap + slot]]


def contract(partners, half_count, *refs):
    places = refs[:half_count]
    pieces = refs[half_count : half_count + len(partners)]
    blocks = refs[half_count + len(partners) : 2 * half_count + len(partners)]
    out_ref, received, stage, sems = refs[2 * half_count + len(partners) :]
    tiles, per_half, inner, columns = blocks[0].shape
    me = lax.axis_index("wide")
    for partner, piece_ref in zip(partners, pieces):
        cap = piece_ref.shape[0]
        received[pl.ds((me ^ partner) * cap, cap)] = piece_ref[...]
    copies = []
    for x in range(tiles):
        total = None
        for place_ref, block_ref in zip(places, blocks):
            picked = jnp.concatenate(
                [received[place_ref[x, k]] for k in range(per_half)], axis=1
            )
            part = jnp.dot(
                picked,
                block_ref[x].reshape(per_half * inner, columns),
                preferred_element_type=jnp.float32,
            )
            total = part if total is None else total + part
        stage[x] = total.astype(stage.dtype)
        copy = pltpu.make_async_copy(stage.at[x], out_ref.at[x], sems.at[x])
        copy.start()
        copies.append(copy)
    for copy in copies:
        copy.wait()


def on_device(wide, narrow, amplitudes, send_list, tile_positions, integrals):
    smem = pl.BlockSpec(memory_space=pltpu.SMEM)
    vmem = pl.BlockSpec(memory_space=pltpu.VMEM)
    anywhere = pl.BlockSpec(memory_space=pl.ANY)
    hbm = pl.BlockSpec(memory_space=pltpu.HBM)
    params = pltpu.CompilerParams(vmem_limit_bytes=VMEM_LIMIT)
    cap = send_list.shape[1] // wide
    pairs, columns = amplitudes.shape[1:]
    tiles = integrals.shape[0]
    piece = jax.ShapeDtypeStruct((cap, pairs, columns), amplitudes.dtype)
    partners = tuple(range(wide - 1, -1, -1))
    outgoing = pl.pallas_call(
        functools.partial(pick_outgoing, partners),
        out_shape=[piece] * wide,
        in_specs=[hbm, hbm],
        out_specs=[vmem] * wide,
        scratch_shapes=[
            pltpu.SMEM(send_list.shape, send_list.dtype),
            pltpu.VMEM(amplitudes.shape, amplitudes.dtype),
            pltpu.SemaphoreType.DMA((2,)),
        ],
        compiler_params=params,
    )(send_list, amplitudes)
    if wide <= DIRECT_WIDE:
        pieces = [
            lax.ppermute(sent, "wide", [(d, d ^ partner) for d in range(wide)]) if partner else sent
            for partner, sent in zip(partners, outgoing)
        ]
    else:
        me = lax.axis_index("wide")
        stacked = jnp.stack(outgoing[::-1])[jnp.arange(wide) ^ me]
        arrived = lax.all_to_all(stacked, "wide", split_axis=0, concat_axis=0, tiled=True)
        arrived = arrived[jnp.arange(wide) ^ me]
        pieces = [arrived[partner] for partner in partners]
    if narrow == 2:
        swap = [(0, 1), (1, 0)]
        places = [tile_positions, lax.ppermute(tile_positions, "narrow", swap)]
        blocks = [integrals, lax.ppermute(integrals, "narrow", swap)]
    else:
        places = [lax.all_gather(tile_positions, "narrow", axis=1, tiled=True)]
        blocks = [lax.all_gather(integrals, "narrow", axis=1, tiled=True)]
    count = len(blocks)
    return pl.pallas_call(
        functools.partial(contract, partners, count),
        out_shape=jax.ShapeDtypeStruct((tiles, pairs, columns), jnp.bfloat16),
        in_specs=[smem] * count + [vmem] * (count + wide),
        out_specs=anywhere,
        scratch_shapes=[
            pltpu.VMEM((cap * wide, pairs, columns), amplitudes.dtype),
            pltpu.VMEM((tiles, pairs, columns), jnp.bfloat16),
            pltpu.SemaphoreType.DMA((tiles,)),
        ],
        compiler_params=params,
    )(*places, *pieces, *blocks)


def solution(mesh):
    placed = (
        P("wide", "narrow", None),
        P("wide", None),
        P("wide", "narrow"),
        P("wide", "narrow", None, None),
    )
    return jax.shard_map(
        functools.partial(on_device, mesh.shape["wide"], mesh.shape["narrow"]),
        mesh=mesh,
        in_specs=placed,
        out_specs=P("wide", "narrow", None),
        check_vma=False,
    )
```

```python
import functools

import jax
import jax.numpy as jnp
from jax import lax
from jax.experimental import pallas as pl
from jax.experimental.pallas import tpu as pltpu
from jax.sharding import PartitionSpec as P

VMEM_LIMIT = 48 * 1024 * 1024
SMEM = pl.BlockSpec(memory_space=pltpu.SMEM)
VMEM = pl.BlockSpec(memory_space=pltpu.VMEM)
ANYWHERE = pl.BlockSpec(memory_space=pl.ANY)
PARAMS = pltpu.CompilerParams(vmem_limit_bytes=VMEM_LIMIT)


def device_of(me, half, spot):
    return ((me // half[0] + half[1]) % 2) * half[0] + spot


def pick_outgoing(plan, near, cap, send_ref, amplitudes_ref, *refs):
    out_refs = refs[: len(plan)]
    sends, held, sems = refs[len(plan) :]
    fetch_sends = pltpu.make_async_copy(send_ref, sends, sems.at[0])
    fetch_tiles = pltpu.make_async_copy(amplitudes_ref, held, sems.at[1])
    fetch_sends.start()
    fetch_tiles.start()
    fetch_sends.wait()
    fetch_tiles.wait()
    me = lax.axis_index("wide")
    for wanted, out_ref in zip(plan, out_refs):
        for place, (half, spot, slot) in enumerate(wanted):
            out_ref[place] = held[sends[0, device_of(me, (near, half), spot) * cap + slot]]


def take_crossing(count, both_ref, out_ref):
    for spot in range(out_ref.shape[0] // count):
        out_ref[pl.ds(spot * count, count)] = both_ref[pl.ds((2 * spot + 1) * count, count)]


def join_halves(count, own_ref, crossed_ref, out_ref):
    for spot in range(own_ref.shape[0] // count):
        here = pl.ds(spot * count, count)
        out_ref[pl.ds(2 * spot * count, count)] = own_ref[here]
        out_ref[pl.ds((2 * spot + 1) * count, count)] = crossed_ref[here]


def stage_own(after_ref, places_ref, blocks_ref, places_out, blocks_out, sems):
    copies = [
        pltpu.make_async_copy(places_ref, places_out, sems.at[0]),
        pltpu.make_async_copy(blocks_ref, blocks_out, sems.at[1]),
    ]
    for copy in copies:
        copy.start()
    for copy in copies:
        copy.wait()


def contract(plan, near, cap, half_count, *refs):
    places = refs[:half_count]
    pieces = refs[half_count : half_count + len(plan)]
    blocks = refs[half_count + len(plan) : 2 * half_count + len(plan)]
    out_ref, received, stage, sems = refs[2 * half_count + len(plan) :]
    tiles, per_half, inner, columns = blocks[0].shape
    me = lax.axis_index("wide")
    for origin, piece_ref in zip(plan, pieces):
        for place, spot in origin:
            half, device, slot = spot
            received[device_of(me, (near, half), device) * cap + slot] = piece_ref[place]
    copies = []
    for x in range(tiles):
        total = None
        for place_ref, block_ref in zip(places, blocks):
            picked = jnp.concatenate(
                [received[place_ref[x, k]] for k in range(per_half)], axis=1
            )
            part = jnp.dot(
                picked,
                block_ref[x].reshape(per_half * inner, columns),
                preferred_element_type=jnp.float32,
            )
            total = part if total is None else total + part
        stage[x] = total.astype(stage.dtype)
        copy = pltpu.make_async_copy(stage.at[x], out_ref.at[x], sems.at[x])
        copy.start()
        copies.append(copy)
    for copy in copies:
        copy.wait()


def rearranged(body, shape, *arrays):
    return pl.pallas_call(
        body,
        out_shape=jax.ShapeDtypeStruct(shape, arrays[0].dtype),
        in_specs=[VMEM] * len(arrays),
        out_specs=VMEM,
        compiler_params=PARAMS,
    )(*arrays)


def on_device(wide, narrow, amplitudes, send_list, tile_positions, integrals):
    cap = send_list.shape[1] // wide
    pairs, columns = amplitudes.shape[1:]
    tiles = integrals.shape[0]
    near = wide // 2
    early, late = range(cap // 2), range(cap // 2, cap)
    groups = [list(range(near)), list(range(near, wide))]
    opposite = [(d, (d + near) % wide) for d in range(wide)]

    def cross(array):
        return lax.ppermute(array, "wide", opposite)

    def spread(array):
        return lax.all_to_all(
            array, "wide", split_axis=0, concat_axis=0, axis_index_groups=groups, tiled=True
        )

    def both(slots):
        return [(half, spot, slot) for spot in range(near) for half in (0, 1) for slot in slots]

    asked = [
        [(1, spot, slot) for spot in range(near) for slot in early],
        both(late),
        [(0, spot, slot) for spot in range(near) for slot in early],
    ]
    cross_first, spread_first, kept = pl.pallas_call(
        functools.partial(pick_outgoing, asked, near, cap),
        out_shape=[jax.ShapeDtypeStruct((len(p), pairs, columns), amplitudes.dtype) for p in asked],
        in_specs=[ANYWHERE, ANYWHERE],
        out_specs=[VMEM] * len(asked),
        scratch_shapes=[
            pltpu.SMEM(send_list.shape, send_list.dtype),
            pltpu.VMEM(amplitudes.shape, amplitudes.dtype),
            pltpu.SemaphoreType.DMA((2,)),
        ],
        compiler_params=PARAMS,
    )(send_list, amplitudes)
    tile = (pairs, columns)
    crossed = cross(cross_first)
    spread_late = spread(spread_first)
    second = rearranged(functools.partial(take_crossing, len(late)), (near * len(late),) + tile, spread_late)
    crossed_late = cross(second)
    joined = rearranged(
        functools.partial(join_halves, len(early)), (2 * near * len(early),) + tile, kept, crossed
    )
    spread_early = spread(joined)
    pieces = [spread_late, crossed_late, spread_early]
    plan = [
        [(i, place) for i, place in enumerate(both(late)) if place[0] == 0],
        list(enumerate((1, spot, slot) for spot in range(near) for slot in late)),
        list(enumerate(both(early))),
    ]
    tied, started = lax.optimization_barrier((integrals, second))
    staged = pl.pallas_call(
        stage_own,
        out_shape=[
            jax.ShapeDtypeStruct(tile_positions.shape, tile_positions.dtype),
            jax.ShapeDtypeStruct(integrals.shape, integrals.dtype),
        ],
        in_specs=[ANYWHERE] * 3,
        out_specs=[VMEM, VMEM],
        scratch_shapes=[pltpu.SemaphoreType.DMA((2,))],
        compiler_params=PARAMS,
        cost_estimate=pl.CostEstimate(flops=0, bytes_accessed=2 * integrals.size * 2, transcendentals=0),
    )
    if narrow == 2:
        swap = [(0, 1), (1, 0)]
        own_places, own_blocks = staged(started, tile_positions, tied)
        places = [own_places, lax.ppermute(tile_positions, "narrow", swap)]
        blocks = [own_blocks, lax.ppermute(tied, "narrow", swap)]
    else:
        places = [lax.all_gather(tile_positions, "narrow", axis=1, tiled=True)]
        blocks = [lax.all_gather(tied, "narrow", axis=1, tiled=True)]
    count = len(blocks)
    return pl.pallas_call(
        functools.partial(contract, plan, near, cap, count),
        out_shape=jax.ShapeDtypeStruct((tiles, pairs, columns), jnp.bfloat16),
        in_specs=[SMEM] * count + [VMEM] * (count + len(pieces)),
        out_specs=ANYWHERE,
        scratch_shapes=[
            pltpu.VMEM((cap * wide, pairs, columns), amplitudes.dtype),
            pltpu.VMEM((tiles, pairs, columns), jnp.bfloat16),
            pltpu.SemaphoreType.DMA((tiles,)),
        ],
        compiler_params=PARAMS,
    )(*places, *pieces, *blocks)


def solution(mesh):
    placed = (
        P("wide", "narrow", None),
        P("wide", None),
        P("wide", "narrow"),
        P("wide", "narrow", None, None),
    )
    return jax.shard_map(
        functools.partial(on_device, mesh.shape["wide"], mesh.shape["narrow"]),
        mesh=mesh,
        in_specs=placed,
        out_specs=P("wide", "narrow", None),
        check_vma=False,
    )
```

```python
import functools

import jax
import jax.numpy as jnp
from jax import lax
from jax.experimental import pallas as pl
from jax.experimental.pallas import tpu as pltpu
from jax.sharding import PartitionSpec as P

VMEM_LIMIT = 48 * 1024 * 1024
SMEM = pl.BlockSpec(memory_space=pltpu.SMEM)
VMEM = pl.BlockSpec(memory_space=pltpu.VMEM)
ANYWHERE = pl.BlockSpec(memory_space=pl.ANY)
PARAMS = pltpu.CompilerParams(vmem_limit_bytes=VMEM_LIMIT)


def device_of(me, half, spot):
    return ((me // half[0] + half[1]) % 2) * half[0] + spot


def pick_outgoing(plan, near, cap, send_ref, amplitudes_ref, *refs):
    out_refs = refs[: len(plan)]
    sends, held, sems = refs[len(plan) :]
    fetch_sends = pltpu.make_async_copy(send_ref, sends, sems.at[0])
    fetch_tiles = pltpu.make_async_copy(amplitudes_ref, held, sems.at[1])
    fetch_sends.start()
    fetch_tiles.start()
    fetch_sends.wait()
    fetch_tiles.wait()
    me = lax.axis_index("wide")
    for wanted, out_ref in zip(plan, out_refs):
        for place, (half, spot, slot) in enumerate(wanted):
            out_ref[place] = held[sends[0, device_of(me, (near, half), spot) * cap + slot]]


def take_crossing(count, both_ref, out_ref):
    for spot in range(out_ref.shape[0] // count):
        out_ref[pl.ds(spot * count, count)] = both_ref[pl.ds((2 * spot + 1) * count, count)]


def join_halves(count, own_ref, crossed_ref, out_ref):
    for spot in range(own_ref.shape[0] // count):
        here = pl.ds(spot * count, count)
        out_ref[pl.ds(2 * spot * count, count)] = own_ref[here]
        out_ref[pl.ds((2 * spot + 1) * count, count)] = crossed_ref[here]


def contract(plan, near, cap, half_count, *refs):
    places = refs[:half_count]
    pieces = refs[half_count : half_count + len(plan)]
    blocks = refs[half_count + len(plan) : 2 * half_count + len(plan)]
    out_ref, received, stage, out_sems, in_sems = refs[2 * half_count + len(plan) :][:5]
    fetched = refs[2 * half_count + len(plan) + 5 :]
    tiles, per_half, inner, columns = blocks[0].shape
    fetches = [
        [
            pltpu.make_async_copy(block_ref.at[x], held.at[x], in_sems.at[half, x])
            for half, (block_ref, held) in enumerate(zip(blocks, fetched))
        ]
        for x in range(tiles)
    ]
    for fetch in sum(fetches, []):
        fetch.start()
    me = lax.axis_index("wide")
    for origin, piece_ref in zip(plan, pieces):
        for place, spot in origin:
            half, device, slot = spot
            received[device_of(me, (near, half), device) * cap + slot] = piece_ref[place]
    copies = []
    for x in range(tiles):
        total = None
        for place_ref, block_ref, fetch in zip(places, fetched, fetches[x]):
            fetch.wait()
            picked = jnp.concatenate(
                [received[place_ref[x, k]] for k in range(per_half)], axis=1
            )
            part = jnp.dot(
                picked,
                block_ref[x].reshape(per_half * inner, columns),
                preferred_element_type=jnp.float32,
            )
            total = part if total is None else total + part
        stage[x] = total.astype(stage.dtype)
        copy = pltpu.make_async_copy(stage.at[x], out_ref.at[x], out_sems.at[x])
        copy.start()
        copies.append(copy)
    for copy in copies:
        copy.wait()


def rearranged(body, shape, *arrays):
    return pl.pallas_call(
        body,
        out_shape=jax.ShapeDtypeStruct(shape, arrays[0].dtype),
        in_specs=[VMEM] * len(arrays),
        out_specs=VMEM,
        compiler_params=PARAMS,
    )(*arrays)


def on_device(wide, narrow, amplitudes, send_list, tile_positions, integrals):
    cap = send_list.shape[1] // wide
    pairs, columns = amplitudes.shape[1:]
    tiles = integrals.shape[0]
    near = wide // 2
    early, late = range(cap // 2), range(cap // 2, cap)
    groups = [list(range(near)), list(range(near, wide))]
    opposite = [(d, (d + near) % wide) for d in range(wide)]

    def cross(array):
        return lax.ppermute(array, "wide", opposite)

    def spread(array):
        return lax.all_to_all(
            array, "wide", split_axis=0, concat_axis=0, axis_index_groups=groups, tiled=True
        )

    def both(slots):
        return [(half, spot, slot) for spot in range(near) for half in (0, 1) for slot in slots]

    asked = [
        [(1, spot, slot) for spot in range(near) for slot in early],
        both(late),
        [(0, spot, slot) for spot in range(near) for slot in early],
    ]
    cross_first, spread_first, kept = pl.pallas_call(
        functools.partial(pick_outgoing, asked, near, cap),
        out_shape=[jax.ShapeDtypeStruct((len(p), pairs, columns), amplitudes.dtype) for p in asked],
        in_specs=[ANYWHERE, ANYWHERE],
        out_specs=[VMEM] * len(asked),
        scratch_shapes=[
            pltpu.SMEM(send_list.shape, send_list.dtype),
            pltpu.VMEM(amplitudes.shape, amplitudes.dtype),
            pltpu.SemaphoreType.DMA((2,)),
        ],
        compiler_params=PARAMS,
    )(send_list, amplitudes)
    tile = (pairs, columns)
    crossed = cross(cross_first)
    spread_late = spread(spread_first)
    second = rearranged(functools.partial(take_crossing, len(late)), (near * len(late),) + tile, spread_late)
    crossed_late = cross(second)
    joined = rearranged(
        functools.partial(join_halves, len(early)), (2 * near * len(early),) + tile, kept, crossed
    )
    spread_early = spread(joined)
    pieces = [spread_late, crossed_late, spread_early]
    plan = [
        [(i, place) for i, place in enumerate(both(late)) if place[0] == 0],
        list(enumerate((1, spot, slot) for spot in range(near) for slot in late)),
        list(enumerate(both(early))),
    ]
    if narrow == 2:
        swap = [(0, 1), (1, 0)]
        places = [tile_positions, lax.ppermute(tile_positions, "narrow", swap)]
        blocks = [integrals, lax.ppermute(integrals, "narrow", swap)]
    else:
        places = [lax.all_gather(tile_positions, "narrow", axis=1, tiled=True)]
        blocks = [lax.all_gather(integrals, "narrow", axis=1, tiled=True)]
    count = len(blocks)
    return pl.pallas_call(
        functools.partial(contract, plan, near, cap, count),
        out_shape=jax.ShapeDtypeStruct((tiles, pairs, columns), jnp.bfloat16),
        in_specs=[SMEM] * count + [VMEM] * len(pieces) + [ANYWHERE] * count,
        out_specs=ANYWHERE,
        scratch_shapes=[
            pltpu.VMEM((cap * wide, pairs, columns), amplitudes.dtype),
            pltpu.VMEM((tiles, pairs, columns), jnp.bfloat16),
            pltpu.SemaphoreType.DMA((tiles,)),
            pltpu.SemaphoreType.DMA((count, tiles)),
        ]
        + [pltpu.VMEM(block.shape, block.dtype) for block in blocks],
        compiler_params=PARAMS,
    )(*places, *pieces, *blocks)


def solution(mesh):
    placed = (
        P("wide", "narrow", None),
        P("wide", None),
        P("wide", "narrow"),
        P("wide", "narrow", None, None),
    )
    return jax.shard_map(
        functools.partial(on_device, mesh.shape["wide"], mesh.shape["narrow"]),
        mesh=mesh,
        in_specs=placed,
        out_specs=P("wide", "narrow", None),
        check_vma=False,
    )
```

```python
import functools

import jax
import jax.numpy as jnp
from jax import lax
from jax.experimental import pallas as pl
from jax.experimental.pallas import tpu as pltpu
from jax.sharding import PartitionSpec as P

VMEM_LIMIT = 48 * 1024 * 1024
PICK_GRANT = 62 * 1024 * 1024


def pick_outgoing(send_ref, amplitudes_ref, out_ref, sends, send_sem, sems):
    fetch = pltpu.make_async_copy(send_ref, sends, send_sem)
    fetch.start()
    fetch.wait()
    copies = []
    for slot in range(out_ref.shape[0]):
        copy = pltpu.make_async_copy(
            amplitudes_ref.at[sends[0, slot]], out_ref.at[slot], sems.at[slot]
        )
        copy.start()
        copies.append(copy)
    for copy in copies:
        copy.wait()


def contract(half_count, *refs):
    places = refs[:half_count]
    received_ref = refs[half_count]
    blocks = refs[half_count + 1 : 2 * half_count + 1]
    out_ref, stage, sems = refs[2 * half_count + 1 :]
    tiles, per_half, inner, columns = blocks[0].shape
    copies = []
    for x in range(tiles):
        total = None
        for place_ref, block_ref in zip(places, blocks):
            picked = jnp.concatenate(
                [received_ref[place_ref[x, k]] for k in range(per_half)], axis=1
            )
            part = jnp.dot(
                picked,
                block_ref[x].reshape(per_half * inner, columns),
                preferred_element_type=jnp.float32,
            )
            total = part if total is None else total + part
        stage[x] = total.astype(stage.dtype)
        copy = pltpu.make_async_copy(stage.at[x], out_ref.at[x], sems.at[x])
        copy.start()
        copies.append(copy)
    for copy in copies:
        copy.wait()


def on_device(narrow, amplitudes, send_list, tile_positions, integrals):
    smem = pl.BlockSpec(memory_space=pltpu.SMEM)
    anywhere = pl.BlockSpec(memory_space=pl.ANY)
    vmem = pl.BlockSpec(memory_space=pltpu.VMEM)
    params = pltpu.CompilerParams(vmem_limit_bytes=VMEM_LIMIT)
    slots = send_list.shape[1]
    tile_bytes = amplitudes.shape[1] * amplitudes.shape[2] * 2
    outgoing = pl.pallas_call(
        pick_outgoing,
        out_shape=jax.ShapeDtypeStruct((slots,) + amplitudes.shape[1:], amplitudes.dtype),
        in_specs=[anywhere, anywhere],
        out_specs=anywhere,
        scratch_shapes=[
            pltpu.SMEM(send_list.shape, send_list.dtype),
            pltpu.SemaphoreType.DMA,
            pltpu.SemaphoreType.DMA((slots,)),
        ],
        compiler_params=pltpu.CompilerParams(vmem_limit_bytes=PICK_GRANT),
        cost_estimate=pl.CostEstimate(flops=0, bytes_accessed=2 * slots * tile_bytes, transcendentals=0),
    )(send_list, amplitudes)
    if narrow == 2:
        swap = [(0, 1), (1, 0)]
        places = [tile_positions, lax.ppermute(tile_positions, "narrow", swap)]
        blocks = [integrals, lax.ppermute(integrals, "narrow", swap)]
    else:
        places = [lax.all_gather(tile_positions, "narrow", axis=1, tiled=True)]
        blocks = [lax.all_gather(integrals, "narrow", axis=1, tiled=True)]
    received = lax.all_to_all(outgoing, "wide", split_axis=0, concat_axis=0, tiled=True)
    tiles, pairs, columns = integrals.shape[0], amplitudes.shape[1], integrals.shape[3]
    count = len(blocks)
    return pl.pallas_call(
        functools.partial(contract, count),
        out_shape=jax.ShapeDtypeStruct((tiles, pairs, columns), jnp.bfloat16),
        in_specs=[smem] * count + [vmem] * (count + 1),
        out_specs=pl.BlockSpec(memory_space=pl.ANY),
        scratch_shapes=[
            pltpu.VMEM((tiles, pairs, columns), jnp.bfloat16),
            pltpu.SemaphoreType.DMA((tiles,)),
        ],
        compiler_params=params,
    )(*places, received, *blocks)


def solution(mesh):
    placed = (
        P("wide", "narrow", None),
        P("wide", None),
        P("wide", "narrow"),
        P("wide", "narrow", None, None),
    )
    return jax.shard_map(
        functools.partial(on_device, mesh.shape["narrow"]),
        mesh=mesh,
        in_specs=placed,
        out_specs=P("wide", "narrow", None),
        check_vma=False,
    )
```

```python
import functools

import jax
import jax.numpy as jnp
from jax import lax
from jax.experimental import pallas as pl
from jax.experimental.pallas import tpu as pltpu
from jax.sharding import PartitionSpec as P

VMEM_LIMIT = 48 * 1024 * 1024
PICK_GRANT = 62 * 1024 * 1024


def pick_outgoing(send_ref, amplitudes_ref, out_ref, sends, held, in_sems, sems):
    fetch_sends = pltpu.make_async_copy(send_ref, sends, in_sems.at[0])
    fetch_tiles = pltpu.make_async_copy(amplitudes_ref, held, in_sems.at[1])
    fetch_tiles.start()
    fetch_sends.start()
    fetch_sends.wait()
    fetch_tiles.wait()
    copies = []
    for slot in range(out_ref.shape[0]):
        copy = pltpu.make_async_copy(
            held.at[sends[0, slot]], out_ref.at[slot], sems.at[slot]
        )
        copy.start()
        copies.append(copy)
    for copy in copies:
        copy.wait()


def contract(count, *refs):
    places = refs[:count]
    received_ref = refs[count]
    blocks = list(refs[count + 1 : 2 * count + 1])
    out_ref, stage, out_sems, held, in_sems = refs[2 * count + 1 :]
    tiles, per_block, inner, columns = blocks[0].shape
    fetches = [pltpu.make_async_copy(blocks[-1].at[x], held.at[x], in_sems.at[x]) for x in range(tiles)]
    for fetch in fetches:
        fetch.start()
    blocks[-1] = held
    copies = []
    for x in range(tiles):
        total = None
        for number, (place_ref, block_ref) in enumerate(zip(places, blocks)):
            picked = jnp.concatenate(
                [received_ref[place_ref[x, k]] for k in range(per_block)], axis=1
            )
            if number == count - 1:
                fetches[x].wait()
            part = jnp.dot(
                picked,
                block_ref[x].reshape(per_block * inner, columns),
                preferred_element_type=jnp.float32,
            )
            total = part if total is None else total + part
        stage[x] = total.astype(stage.dtype)
        copy = pltpu.make_async_copy(stage.at[x], out_ref.at[x], out_sems.at[x])
        copy.start()
        copies.append(copy)
    for copy in copies:
        copy.wait()


def on_device(narrow, amplitudes, send_list, tile_positions, integrals):
    smem = pl.BlockSpec(memory_space=pltpu.SMEM)
    anywhere = pl.BlockSpec(memory_space=pl.ANY)
    vmem = pl.BlockSpec(memory_space=pltpu.VMEM)
    params = pltpu.CompilerParams(vmem_limit_bytes=VMEM_LIMIT)
    slots = send_list.shape[1]
    tile_bytes = amplitudes.shape[1] * amplitudes.shape[2] * 2
    outgoing = pl.pallas_call(
        pick_outgoing,
        out_shape=jax.ShapeDtypeStruct((slots,) + amplitudes.shape[1:], amplitudes.dtype),
        in_specs=[anywhere, anywhere],
        out_specs=anywhere,
        scratch_shapes=[
            pltpu.SMEM(send_list.shape, send_list.dtype),
            pltpu.VMEM(amplitudes.shape, amplitudes.dtype),
            pltpu.SemaphoreType.DMA((2,)),
            pltpu.SemaphoreType.DMA((slots,)),
        ],
        compiler_params=pltpu.CompilerParams(vmem_limit_bytes=PICK_GRANT),
        cost_estimate=pl.CostEstimate(flops=0, bytes_accessed=2 * slots * tile_bytes, transcendentals=0),
    )(send_list, amplitudes)
    if narrow == 2:
        swap = [(0, 1), (1, 0)]
        places = [tile_positions, lax.ppermute(tile_positions, "narrow", swap)]
        blocks = [integrals, lax.ppermute(integrals, "narrow", swap)]
    else:
        places = [lax.all_gather(tile_positions, "narrow", axis=1, tiled=True)]
        blocks = [lax.all_gather(integrals, "narrow", axis=1, tiled=True)]
    received = lax.all_to_all(outgoing, "wide", split_axis=0, concat_axis=0, tiled=True)
    tiles, pairs, columns = integrals.shape[0], amplitudes.shape[1], integrals.shape[3]
    count = len(blocks)
    return pl.pallas_call(
        functools.partial(contract, count),
        out_shape=jax.ShapeDtypeStruct((tiles, pairs, columns), jnp.bfloat16),
        in_specs=[smem] * count + [vmem] * count + [anywhere],
        out_specs=pl.BlockSpec(memory_space=pl.ANY),
        scratch_shapes=[
            pltpu.VMEM((tiles, pairs, columns), jnp.bfloat16),
            pltpu.SemaphoreType.DMA((tiles,)),
            pltpu.VMEM(blocks[-1].shape, blocks[-1].dtype),
            pltpu.SemaphoreType.DMA((tiles,)),
        ],
        compiler_params=params,
    )(*places, received, *blocks)


def solution(mesh):
    placed = (
        P("wide", "narrow", None),
        P("wide", None),
        P("wide", "narrow"),
        P("wide", "narrow", None, None),
    )
    return jax.shard_map(
        functools.partial(on_device, mesh.shape["narrow"]),
        mesh=mesh,
        in_specs=placed,
        out_specs=P("wide", "narrow", None),
        check_vma=False,
    )
```

```python
import functools
import math

import jax
import jax.numpy as jnp
from jax import lax
from jax.experimental import pallas as pl
from jax.experimental.pallas import tpu as pltpu
from jax.sharding import PartitionSpec as P

SMEM = pl.BlockSpec(memory_space=pltpu.SMEM)
VMEM = pl.BlockSpec(memory_space=pltpu.VMEM)
ANYWHERE = pl.BlockSpec(memory_space=pl.ANY)


GRANT = pltpu.CompilerParams(vmem_limit_bytes=48 * 1024 * 1024)


def pick_outgoing(plan, cap, send_ref, amplitudes_ref, *refs):
    out_refs = refs[: len(plan)]
    sends, held, sems = refs[len(plan) :]
    fetch_sends = pltpu.make_async_copy(send_ref, sends, sems.at[0])
    fetch_tiles = pltpu.make_async_copy(amplitudes_ref, held, sems.at[1])
    fetch_tiles.start()
    fetch_sends.start()
    fetch_sends.wait()
    fetch_tiles.wait()
    me = lax.axis_index("wide")
    for wanted, out_ref in zip(plan, out_refs):
        for place, (partner, slot) in enumerate(wanted):
            out_ref[place] = held[sends[0, (me ^ partner) * cap + slot]]


def regroup(ins, width, staged, *refs):
    in_refs, stage_in = refs[:ins], refs[ins : ins + staged]
    out_refs = refs[ins + staged :]
    copies = []
    if staged:
        out_refs, stage_out, sems = out_refs[: -staged - 1], out_refs[-staged - 1 : -1], out_refs[-1]
        for number in range(staged):
            copy = pltpu.make_async_copy(stage_in[number], stage_out[number], sems.at[number])
            copy.start()
            copies.append(copy)
    for j, out_ref in enumerate(out_refs):
        for i, in_ref in enumerate(in_refs):
            out_ref[i * width : (i + 1) * width] = in_ref[(j + 1) * width : (j + 2) * width]
    for copy in copies:
        copy.wait()


def contract(plan, cap, count, *refs):
    places = refs[:count]
    pieces = refs[count : count + len(plan)]
    blocks = list(refs[count + len(plan) : 2 * count + len(plan)])
    out_ref, received, stage, sems = refs[2 * count + len(plan) :]
    tiles, per_block, inner, columns = blocks[0].shape
    me = lax.axis_index("wide")
    for origin, piece_ref in zip(plan, pieces):
        for place, (partner, slot) in origin:
            received[(me ^ partner) * cap + slot] = piece_ref[place]
    copies = []
    for x in range(tiles):
        total = None
        for place_ref, block_ref in zip(places, blocks):
            picked = jnp.concatenate(
                [received[place_ref[x, k]] for k in range(per_block)], axis=1
            )
            part = jnp.dot(
                picked,
                block_ref[x].reshape(per_block * inner, columns),
                preferred_element_type=jnp.float32,
            )
            total = part if total is None else total + part
        stage[x] = total.astype(stage.dtype)
        copy = pltpu.make_async_copy(stage.at[x], out_ref.at[x], sems.at[x])
        copy.start()
        copies.append(copy)
    for copy in copies:
        copy.wait()


def regrouped(arrays, width, count, staged=()):
    shape = jax.ShapeDtypeStruct((len(arrays) * width,) + arrays[0].shape[1:], arrays[0].dtype)
    outs = pl.pallas_call(
        functools.partial(regroup, len(arrays), width, len(staged)),
        out_shape=[shape] * count + [jax.ShapeDtypeStruct(s.shape, s.dtype) for s in staged],
        in_specs=[VMEM] * len(arrays) + [ANYWHERE] * len(staged),
        out_specs=[VMEM] * (count + len(staged)),
        scratch_shapes=[pltpu.SemaphoreType.DMA((len(staged),))] if staged else [],
        compiler_params=GRANT,
    )(*arrays, *staged)
    return list(outs[:count]), list(outs[count:])


def on_device(wide, narrow, amplitudes, send_list, tile_positions, integrals):
    cap = send_list.shape[1] // wide
    pairs, columns = amplitudes.shape[1:]
    tiles = integrals.shape[0]
    near = math.isqrt(wide)
    far = wide // near
    early, late = range(cap // 2), range(cap // 2, cap)

    def exchange(array, partner):
        return lax.ppermute(array, "wide", [(d, d ^ partner) for d in range(wide)])

    along = [[(a + near * b, s) for a in range(near) for s in early] for b in range(far)]
    across = [[(a + near * b, s) for b in range(far) for s in late] for a in range(near)]
    plan = along + across
    outgoing = pl.pallas_call(
        functools.partial(pick_outgoing, plan, cap),
        out_shape=[jax.ShapeDtypeStruct((len(p), pairs, columns), amplitudes.dtype) for p in plan],
        in_specs=[ANYWHERE, ANYWHERE],
        out_specs=[VMEM] * len(plan),
        scratch_shapes=[
            pltpu.SMEM(send_list.shape, send_list.dtype),
            pltpu.VMEM(amplitudes.shape, amplitudes.dtype),
            pltpu.SemaphoreType.DMA((2,)),
        ],
        compiler_params=GRANT,
    )(send_list, amplitudes)
    if narrow == 2:
        swap = [(0, 1), (1, 0)]
        places = [tile_positions, lax.ppermute(tile_positions, "narrow", swap)]
        blocks = [integrals, lax.ppermute(integrals, "narrow", swap)]
    else:
        places = [lax.all_gather(tile_positions, "narrow", axis=1, tiled=True)]
        blocks = [lax.all_gather(integrals, "narrow", axis=1, tiled=True)]
    first_along, first_across = outgoing[:far], outgoing[far:]
    got_across = [first_across[0]] + [None] * (near - 1)
    got_along = [first_along[0]] + [None] * (far - 1)
    for a in range(near - 1, 0, -1):
        got_across[a] = exchange(first_across[a], a)
    for b in range(far - 1, 0, -1):
        got_along[b] = exchange(first_along[b], near * b)
    second_along, kept = regrouped(got_across, len(late), far - 1, (places[0], blocks[0]) if narrow == 2 else ())
    if narrow == 2:
        places[0], blocks[0] = kept
    second_along, blocks[-1] = lax.optimization_barrier((second_along, blocks[-1]))
    got_along[0], second_along[-1] = lax.optimization_barrier((got_along[0], second_along[-1]))
    last_along = [exchange(second_along[b - 1], near * b) for b in range(far - 1, 0, -1)]
    second_across, _ = regrouped(got_along, len(early), near - 1)
    last_across = [exchange(second_across[a - 1], a) for a in range(near - 1, 0, -1)]
    pieces = got_across + got_along[:1] + got_along[:0:-1] + last_along + last_across
    origins = [list(enumerate((a, s) for s in late)) for a in range(near)]
    origins += [list(enumerate((near * b, s) for s in early)) for b in [0, *range(far - 1, 0, -1)]]
    origins += [list(enumerate((a + near * b, s) for a in range(near) for s in late)) for b in range(far - 1, 0, -1)]
    origins += [list(enumerate((a + near * b, s) for b in range(far) for s in early)) for a in range(near - 1, 0, -1)]
    count = len(blocks)
    return pl.pallas_call(
        functools.partial(contract, origins, cap, count),
        out_shape=jax.ShapeDtypeStruct((tiles, pairs, columns), jnp.bfloat16),
        in_specs=[SMEM] * count + [VMEM] * (len(pieces) + count),
        out_specs=ANYWHERE,
        scratch_shapes=[
            pltpu.VMEM((cap * wide, pairs, columns), amplitudes.dtype),
            pltpu.VMEM((tiles, pairs, columns), jnp.bfloat16),
            pltpu.SemaphoreType.DMA((tiles,)),
        ],
        compiler_params=GRANT,
    )(*places, *pieces, *blocks)


def solution(mesh):
    placed = (
        P("wide", "narrow", None),
        P("wide", None),
        P("wide", "narrow"),
        P("wide", "narrow", None, None),
    )
    return jax.shard_map(
        functools.partial(on_device, mesh.shape["wide"], mesh.shape["narrow"]),
        mesh=mesh,
        in_specs=placed,
        out_specs=P("wide", "narrow", None),
        check_vma=False,
    )
```

```python
import functools

import jax
import jax.numpy as jnp
from jax import lax
from jax.experimental import pallas as pl
from jax.experimental.pallas import tpu as pltpu
from jax.sharding import PartitionSpec as P

SMEM = pl.BlockSpec(memory_space=pltpu.SMEM)
VMEM = pl.BlockSpec(memory_space=pltpu.VMEM)
ANYWHERE = pl.BlockSpec(memory_space=pl.ANY)


GRANT = pltpu.CompilerParams(vmem_limit_bytes=48 * 1024 * 1024)


def pick_outgoing(plan, cap, send_ref, amplitudes_ref, *refs):
    out_refs = refs[: len(plan)]
    sends, held, sems = refs[len(plan) :]
    fetch_sends = pltpu.make_async_copy(send_ref, sends, sems.at[0])
    fetch_tiles = pltpu.make_async_copy(amplitudes_ref, held, sems.at[1])
    fetch_tiles.start()
    fetch_sends.start()
    fetch_sends.wait()
    fetch_tiles.wait()
    me = lax.axis_index("wide")
    for wanted, out_ref in zip(plan, out_refs):
        for place, (partner, slot) in enumerate(wanted):
            out_ref[place] = held[sends[0, (me ^ partner) * cap + slot]]


def take_opposite(count, staged, *refs):
    near_refs, stage_in = refs[:count], refs[count : count + staged]
    out_ref, stage_out, sems = refs[count + staged], refs[count + staged + 1 : count + 2 * staged + 1], refs[-1]
    copies = []
    for number in range(staged):
        copy = pltpu.make_async_copy(stage_in[number], stage_out[number], sems.at[number])
        copy.start()
        copies.append(copy)
    width = out_ref.shape[0] // count
    for spot, near_ref in enumerate(near_refs):
        out_ref[spot * width : (spot + 1) * width] = near_ref[width:]
    for copy in copies:
        copy.wait()


def join_halves(kept_ref, crossed_ref, *out_refs):
    width = out_refs[0].shape[0] // 2
    for spot, out_ref in enumerate(out_refs, 1):
        here = slice(spot * width, (spot + 1) * width)
        out_ref[:width] = kept_ref[here]
        out_ref[width:] = crossed_ref[here]


def contract(plan, cap, count, *refs):
    places = refs[:count]
    pieces = refs[count : count + len(plan)]
    blocks = list(refs[count + len(plan) : 2 * count + len(plan)])
    out_ref, received, stage, sems = refs[2 * count + len(plan) :]
    tiles, per_block, inner, columns = blocks[0].shape
    me = lax.axis_index("wide")
    for origin, piece_ref in zip(plan, pieces):
        for place, (partner, slot) in origin:
            received[(me ^ partner) * cap + slot] = piece_ref[place]
    copies = []
    for x in range(tiles):
        total = None
        for place_ref, block_ref in zip(places, blocks):
            picked = jnp.concatenate(
                [received[place_ref[x, k]] for k in range(per_block)], axis=1
            )
            part = jnp.dot(
                picked,
                block_ref[x].reshape(per_block * inner, columns),
                preferred_element_type=jnp.float32,
            )
            total = part if total is None else total + part
        stage[x] = total.astype(stage.dtype)
        copy = pltpu.make_async_copy(stage.at[x], out_ref.at[x], sems.at[x])
        copy.start()
        copies.append(copy)
    for copy in copies:
        copy.wait()


def on_device(wide, narrow, amplitudes, send_list, tile_positions, integrals):
    cap = send_list.shape[1] // wide
    pairs, columns = amplitudes.shape[1:]
    tiles = integrals.shape[0]
    near = wide // 2
    spots = sorted(range(near), key=lambda a: (a.bit_count(), a))
    early, late = range(cap // 2), range(cap // 2, cap)

    def exchange(array, partner):
        return lax.ppermute(array, "wide", [(d, d ^ partner) for d in range(wide)])

    spread = [[(h * near + a, s) for h in (0, 1) for s in late] for a in spots]
    facing = [(near + a, s) for a in spots for s in early]
    kept = [(a, s) for a in spots for s in early]
    plan = spread + [facing, kept]
    outgoing = pl.pallas_call(
        functools.partial(pick_outgoing, plan, cap),
        out_shape=[jax.ShapeDtypeStruct((len(p), pairs, columns), amplitudes.dtype) for p in plan],
        in_specs=[ANYWHERE, ANYWHERE],
        out_specs=[VMEM] * len(plan),
        scratch_shapes=[
            pltpu.SMEM(send_list.shape, send_list.dtype),
            pltpu.VMEM(amplitudes.shape, amplitudes.dtype),
            pltpu.SemaphoreType.DMA((2,)),
        ],
        compiler_params=GRANT,
    )(send_list, amplitudes)
    if narrow == 2:
        swap = [(0, 1), (1, 0)]
        places = [tile_positions, lax.ppermute(tile_positions, "narrow", swap)]
        blocks = [integrals, lax.ppermute(integrals, "narrow", swap)]
    else:
        places = [lax.all_gather(tile_positions, "narrow", axis=1, tiled=True)]
        blocks = [lax.all_gather(integrals, "narrow", axis=1, tiled=True)]
    cross_first, kept_tiles = outgoing[near:]
    crossed = exchange(cross_first, near)
    spread_late = [outgoing[0]] + [exchange(outgoing[i], a) for i, a in enumerate(spots) if a]
    staged = [places[0], blocks[0]] if narrow == 2 else []
    cross_second, *staged = pl.pallas_call(
        functools.partial(take_opposite, near, len(staged)),
        out_shape=[jax.ShapeDtypeStruct(cross_first.shape, cross_first.dtype)]
        + [jax.ShapeDtypeStruct(s.shape, s.dtype) for s in staged],
        in_specs=[VMEM] * near + [ANYWHERE] * len(staged),
        out_specs=[VMEM] * (1 + len(staged)),
        scratch_shapes=[pltpu.SemaphoreType.DMA((2,))],
        compiler_params=GRANT,
    )(*spread_late, *staged)
    if staged:
        places[0], blocks[0] = staged
    cross_second, blocks[-1], crossed = lax.optimization_barrier((cross_second, blocks[-1])) + (crossed,)
    crossed_late = exchange(cross_second, near)
    joined = pl.pallas_call(
        join_halves,
        out_shape=[jax.ShapeDtypeStruct(outgoing[0].shape, outgoing[0].dtype)] * (near - 1),
        in_specs=[VMEM, VMEM],
        out_specs=[VMEM] * (near - 1),
        compiler_params=GRANT,
    )(kept_tiles, crossed)
    spread_early = [exchange(joined[i - 1], a) for i, a in enumerate(spots) if a]
    pieces = spread_late + [kept_tiles, crossed] + spread_early + [crossed_late]
    origins = [list(enumerate((a, s) for s in late)) for a in spots]
    origins += [list(enumerate((0, s) for s in early)), list(enumerate((near, s) for s in early))]
    origins += [list(enumerate((h * near + a, s) for h in (0, 1) for s in early)) for a in spots[1:]]
    origins += [list(enumerate((near + a, s) for a in spots for s in late))]
    count = len(blocks)
    return pl.pallas_call(
        functools.partial(contract, origins, cap, count),
        out_shape=jax.ShapeDtypeStruct((tiles, pairs, columns), jnp.bfloat16),
        in_specs=[SMEM] * count + [VMEM] * (len(pieces) + count),
        out_specs=ANYWHERE,
        scratch_shapes=[
            pltpu.VMEM((cap * wide, pairs, columns), amplitudes.dtype),
            pltpu.VMEM((tiles, pairs, columns), jnp.bfloat16),
            pltpu.SemaphoreType.DMA((tiles,)),
        ],
        compiler_params=GRANT,
    )(*places, *pieces, *blocks)


def solution(mesh):
    placed = (
        P("wide", "narrow", None),
        P("wide", None),
        P("wide", "narrow"),
        P("wide", "narrow", None, None),
    )
    return jax.shard_map(
        functools.partial(on_device, mesh.shape["wide"], mesh.shape["narrow"]),
        mesh=mesh,
        in_specs=placed,
        out_specs=P("wide", "narrow", None),
        check_vma=False,
    )
```

```python
import functools

import jax
import jax.numpy as jnp
from jax import lax
from jax.experimental import pallas as pl
from jax.experimental.pallas import tpu as pltpu
from jax.sharding import PartitionSpec as P

VMEM_LIMIT = 48 * 1024 * 1024
PICK_GRANT = 62 * 1024 * 1024


def pick_outgoing(send_ref, amplitudes_ref, out_ref, sends, held, in_sems, sems):
    fetch_sends = pltpu.make_async_copy(send_ref, sends, in_sems.at[0])
    fetch_tiles = pltpu.make_async_copy(amplitudes_ref, held, in_sems.at[1])
    fetch_tiles.start()
    fetch_sends.start()
    fetch_sends.wait()
    fetch_tiles.wait()
    copies = []
    for slot in range(out_ref.shape[0]):
        copy = pltpu.make_async_copy(
            held.at[sends[0, slot]], out_ref.at[slot], sems.at[slot]
        )
        copy.start()
        copies.append(copy)
    for copy in copies:
        copy.wait()


def contract(count, *refs):
    places = refs[:count]
    received_ref = refs[count]
    blocks = list(refs[count + 1 : 2 * count + 1])
    out_ref, totals, stage, held, in_sem, out_sem = refs[2 * count + 1 :]
    tiles, per_block, inner, columns = blocks[0].shape
    fetch = pltpu.make_async_copy(blocks[-1], held, in_sem)
    fetch.start()
    blocks[-1] = held
    copies = []
    for number, (place_ref, block_ref) in enumerate(zip(places, blocks)):
        if number == count - 1:
            fetch.wait()
        for x in range(tiles):
            picked = jnp.concatenate(
                [received_ref[place_ref[x, k]] for k in range(per_block)], axis=1
            )
            part = jnp.dot(
                picked,
                block_ref[x].reshape(per_block * inner, columns),
                preferred_element_type=jnp.float32,
            )
            if number:
                part = totals[x] + part
            if number < count - 1:
                totals[x] = part
            else:
                stage[x] = part.astype(stage.dtype)
    copy = pltpu.make_async_copy(stage, out_ref, out_sem)
    copy.start()
    copy.wait()


def on_device(narrow, amplitudes, send_list, tile_positions, integrals):
    smem = pl.BlockSpec(memory_space=pltpu.SMEM)
    anywhere = pl.BlockSpec(memory_space=pl.ANY)
    vmem = pl.BlockSpec(memory_space=pltpu.VMEM)
    params = pltpu.CompilerParams(vmem_limit_bytes=VMEM_LIMIT)
    slots = send_list.shape[1]
    tile_bytes = amplitudes.shape[1] * amplitudes.shape[2] * 2
    outgoing = pl.pallas_call(
        pick_outgoing,
        out_shape=jax.ShapeDtypeStruct((slots,) + amplitudes.shape[1:], amplitudes.dtype),
        in_specs=[anywhere, anywhere],
        out_specs=anywhere,
        scratch_shapes=[
            pltpu.SMEM(send_list.shape, send_list.dtype),
            pltpu.VMEM(amplitudes.shape, amplitudes.dtype),
            pltpu.SemaphoreType.DMA((2,)),
            pltpu.SemaphoreType.DMA((slots,)),
        ],
        compiler_params=pltpu.CompilerParams(vmem_limit_bytes=PICK_GRANT),
        cost_estimate=pl.CostEstimate(flops=0, bytes_accessed=2 * slots * tile_bytes, transcendentals=0),
    )(send_list, amplitudes)
    if narrow == 2:
        swap = [(0, 1), (1, 0)]
        places = [tile_positions, lax.ppermute(tile_positions, "narrow", swap)]
        blocks = [integrals, lax.ppermute(integrals, "narrow", swap)]
    else:
        places = [lax.all_gather(tile_positions, "narrow", axis=1, tiled=True)]
        blocks = [lax.all_gather(integrals, "narrow", axis=1, tiled=True)]
    received = lax.all_to_all(outgoing, "wide", split_axis=0, concat_axis=0, tiled=True)
    tiles, pairs, columns = integrals.shape[0], amplitudes.shape[1], integrals.shape[3]
    count = len(blocks)
    return pl.pallas_call(
        functools.partial(contract, count),
        out_shape=jax.ShapeDtypeStruct((tiles, pairs, columns), jnp.bfloat16),
        in_specs=[smem] * count + [vmem] * count + [anywhere],
        out_specs=pl.BlockSpec(memory_space=pl.ANY),
        scratch_shapes=[
            pltpu.VMEM((tiles, pairs, columns), jnp.float32),
            pltpu.VMEM((tiles, pairs, columns), jnp.bfloat16),
            pltpu.VMEM(blocks[-1].shape, blocks[-1].dtype),
            pltpu.SemaphoreType.DMA,
            pltpu.SemaphoreType.DMA,
        ],
        compiler_params=params,
    )(*places, received, *blocks)


def solution(mesh):
    placed = (
        P("wide", "narrow", None),
        P("wide", None),
        P("wide", "narrow"),
        P("wide", "narrow", None, None),
    )
    return jax.shard_map(
        functools.partial(on_device, mesh.shape["narrow"]),
        mesh=mesh,
        in_specs=placed,
        out_specs=P("wide", "narrow", None),
        check_vma=False,
    )
```

```python
import functools
import math

import jax
import jax.numpy as jnp
from jax import lax
from jax.experimental import pallas as pl
from jax.experimental.pallas import tpu as pltpu
from jax.sharding import PartitionSpec as P

SMEM = pl.BlockSpec(memory_space=pltpu.SMEM)
VMEM = pl.BlockSpec(memory_space=pltpu.VMEM)
ANYWHERE = pl.BlockSpec(memory_space=pl.ANY)


PARTS = 4
LATE = 3
GRANT = pltpu.CompilerParams(vmem_limit_bytes=48 * 1024 * 1024)


def pick_outgoing(plan, cap, send_ref, amplitudes_ref, *refs):
    out_refs = refs[: len(plan)]
    sends, held, sems = refs[len(plan) :]
    fetch_sends = pltpu.make_async_copy(send_ref, sends, sems.at[0])
    fetch_tiles = pltpu.make_async_copy(amplitudes_ref, held, sems.at[1])
    fetch_tiles.start()
    fetch_sends.start()
    fetch_sends.wait()
    fetch_tiles.wait()
    me = lax.axis_index("wide")
    for wanted, out_ref in zip(plan, out_refs):
        rows = out_ref.shape[1]
        for place, (partner, (slot, part)) in enumerate(wanted):
            tile = sends[0, (me ^ partner) * cap + slot]
            out_ref[place] = held[tile, part * rows : (part + 1) * rows]


def regroup(ins, width, staged, *refs):
    in_refs, stage_in = refs[:ins], refs[ins : ins + staged]
    out_refs = refs[ins + staged :]
    copies = []
    if staged:
        out_refs, stage_out, sems = out_refs[: -staged - 1], out_refs[-staged - 1 : -1], out_refs[-1]
        for number in range(staged):
            copy = pltpu.make_async_copy(stage_in[number], stage_out[number], sems.at[number])
            copy.start()
            copies.append(copy)
    for j, out_ref in enumerate(out_refs):
        for i, in_ref in enumerate(in_refs):
            out_ref[i * width : (i + 1) * width] = in_ref[(j + 1) * width : (j + 2) * width]
    for copy in copies:
        copy.wait()


def contract(plan, cap, count, *refs):
    places = refs[:count]
    pieces = refs[count : count + len(plan)]
    blocks = list(refs[count + len(plan) : 2 * count + len(plan)])
    out_ref, received, stage, sems = refs[2 * count + len(plan) :]
    tiles, per_block, inner, columns = blocks[0].shape
    me = lax.axis_index("wide")
    for origin, piece_ref in zip(plan, pieces):
        rows = piece_ref.shape[1]
        for place, (partner, (slot, part)) in origin:
            received[(me ^ partner) * cap + slot, part * rows : (part + 1) * rows] = piece_ref[place]
    copies = []
    for x in range(tiles):
        total = None
        for place_ref, block_ref in zip(places, blocks):
            picked = jnp.concatenate(
                [received[place_ref[x, k]] for k in range(per_block)], axis=1
            )
            part = jnp.dot(
                picked,
                block_ref[x].reshape(per_block * inner, columns),
                preferred_element_type=jnp.float32,
            )
            total = part if total is None else total + part
        stage[x] = total.astype(stage.dtype)
        copy = pltpu.make_async_copy(stage.at[x], out_ref.at[x], sems.at[x])
        copy.start()
        copies.append(copy)
    for copy in copies:
        copy.wait()


def regrouped(arrays, width, count, staged=()):
    shape = jax.ShapeDtypeStruct((len(arrays) * width,) + arrays[0].shape[1:], arrays[0].dtype)
    outs = pl.pallas_call(
        functools.partial(regroup, len(arrays), width, len(staged)),
        out_shape=[shape] * count + [jax.ShapeDtypeStruct(s.shape, s.dtype) for s in staged],
        in_specs=[VMEM] * len(arrays) + [ANYWHERE] * len(staged),
        out_specs=[VMEM] * (count + len(staged)),
        scratch_shapes=[pltpu.SemaphoreType.DMA((len(staged),))] if staged else [],
        compiler_params=GRANT,
    )(*arrays, *staged)
    return list(outs[:count]), list(outs[count:])


def on_device(wide, narrow, amplitudes, send_list, tile_positions, integrals):
    cap = send_list.shape[1] // wide
    pairs, columns = amplitudes.shape[1:]
    tiles = integrals.shape[0]
    near = math.isqrt(wide)
    far = wide // near
    units = [(slot, part) for slot in range(cap) for part in range(PARTS)]
    early, late = units[:-LATE], units[-LATE:]

    def exchange(array, partner):
        return lax.ppermute(array, "wide", [(d, d ^ partner) for d in range(wide)])

    along = [[(a + near * b, s) for a in range(near) for s in early] for b in range(far)]
    across = [[(a + near * b, s) for b in range(far) for s in late] for a in range(near)]
    plan = along + across
    outgoing = pl.pallas_call(
        functools.partial(pick_outgoing, plan, cap),
        out_shape=[jax.ShapeDtypeStruct((len(p), pairs // PARTS, columns), amplitudes.dtype) for p in plan],
        in_specs=[ANYWHERE, ANYWHERE],
        out_specs=[VMEM] * len(plan),
        scratch_shapes=[
            pltpu.SMEM(send_list.shape, send_list.dtype),
            pltpu.VMEM(amplitudes.shape, amplitudes.dtype),
            pltpu.SemaphoreType.DMA((2,)),
        ],
        compiler_params=GRANT,
    )(send_list, amplitudes)
    if narrow == 2:
        swap = [(0, 1), (1, 0)]
        places = [tile_positions, lax.ppermute(tile_positions, "narrow", swap)]
        blocks = [integrals, lax.ppermute(integrals, "narrow", swap)]
    else:
        places = [lax.all_gather(tile_positions, "narrow", axis=1, tiled=True)]
        blocks = [lax.all_gather(integrals, "narrow", axis=1, tiled=True)]
    first_along, first_across = outgoing[:far], outgoing[far:]
    got_across = [first_across[0]] + [None] * (near - 1)
    got_along = [first_along[0]] + [None] * (far - 1)
    for a in range(near - 1, 0, -1):
        got_across[a] = exchange(first_across[a], a)
    for b in range(far - 1, 0, -1):
        got_along[b] = exchange(first_along[b], near * b)
    second_along, kept = regrouped(got_across, len(late), far - 1, (places[0], blocks[0]) if narrow == 2 else ())
    if narrow == 2:
        places[0], blocks[0] = kept
    second_along, blocks[-1] = lax.optimization_barrier((second_along, blocks[-1]))
    got_along[0], second_along[-1] = lax.optimization_barrier((got_along[0], second_along[-1]))
    last_along = [exchange(second_along[b - 1], near * b) for b in range(far - 1, 0, -1)]
    got_along[0], places[-1] = lax.optimization_barrier((got_along[0], places[-1]))
    second_across, _ = regrouped(got_along, len(early), near - 1)
    last_across = [exchange(second_across[a - 1], a) for a in range(near - 1, 0, -1)]
    pieces = got_across + got_along[:1] + got_along[:0:-1] + last_along + last_across
    origins = [list(enumerate((a, s) for s in late)) for a in range(near)]
    origins += [list(enumerate((near * b, s) for s in early)) for b in [0, *range(far - 1, 0, -1)]]
    origins += [list(enumerate((a + near * b, s) for a in range(near) for s in late)) for b in range(far - 1, 0, -1)]
    origins += [list(enumerate((a + near * b, s) for b in range(far) for s in early)) for a in range(near - 1, 0, -1)]
    count = len(blocks)
    return pl.pallas_call(
        functools.partial(contract, origins, cap, count),
        out_shape=jax.ShapeDtypeStruct((tiles, pairs, columns), jnp.bfloat16),
        in_specs=[SMEM] * count + [VMEM] * (len(pieces) + count),
        out_specs=ANYWHERE,
        scratch_shapes=[
            pltpu.VMEM((cap * wide, pairs, columns), amplitudes.dtype),
            pltpu.VMEM((tiles, pairs, columns), jnp.bfloat16),
            pltpu.SemaphoreType.DMA((tiles,)),
        ],
        compiler_params=GRANT,
    )(*places, *pieces, *blocks)


def solution(mesh):
    placed = (
        P("wide", "narrow", None),
        P("wide", None),
        P("wide", "narrow"),
        P("wide", "narrow", None, None),
    )
    return jax.shard_map(
        functools.partial(on_device, mesh.shape["wide"], mesh.shape["narrow"]),
        mesh=mesh,
        in_specs=placed,
        out_specs=P("wide", "narrow", None),
        check_vma=False,
    )
```

```python
import functools
import math

import jax
import jax.numpy as jnp
from jax import lax
from jax.experimental import pallas as pl
from jax.experimental.pallas import tpu as pltpu
from jax.sharding import PartitionSpec as P

SMEM = pl.BlockSpec(memory_space=pltpu.SMEM)
VMEM = pl.BlockSpec(memory_space=pltpu.VMEM)
ANYWHERE = pl.BlockSpec(memory_space=pl.ANY)


PARTS = 4
LATE = 3
GRANT = pltpu.CompilerParams(vmem_limit_bytes=48 * 1024 * 1024)


def pick_outgoing(plan, cap, send_ref, amplitudes_ref, *refs):
    out_refs = refs[: len(plan)]
    sends, held, sems = refs[len(plan) :]
    fetch_sends = pltpu.make_async_copy(send_ref, sends, sems.at[0])
    fetch_tiles = pltpu.make_async_copy(amplitudes_ref, held, sems.at[1])
    fetch_tiles.start()
    fetch_sends.start()
    fetch_sends.wait()
    fetch_tiles.wait()
    me = lax.axis_index("wide")
    for wanted, out_ref in zip(plan, out_refs):
        rows = out_ref.shape[1]
        for place, (relative, partner, (slot, part)) in enumerate(wanted):
            tile = sends[0, (relative * me ^ partner) * cap + slot]
            out_ref[place] = held[tile, part * rows : (part + 1) * rows]


def regroup(ins, width, *refs):
    in_refs, out_refs = refs[:ins], refs[ins:]
    for j, out_ref in enumerate(out_refs):
        for i, in_ref in enumerate(in_refs):
            out_ref[i * width : (i + 1) * width] = in_ref[(j + 1) * width : (j + 2) * width]


def contract(plan, cap, count, *refs):
    places = refs[:count]
    pieces = refs[count : count + len(plan)]
    blocks = list(refs[count + len(plan) : 2 * count + len(plan)])
    out_ref, received, stage, sems = refs[2 * count + len(plan) :]
    tiles, per_block, inner, columns = blocks[0].shape
    me = lax.axis_index("wide")
    for origin, piece_ref in zip(plan, pieces):
        rows = piece_ref.shape[1]
        for place, (relative, partner, (slot, part)) in origin:
            received[(relative * me ^ partner) * cap + slot, part * rows : (part + 1) * rows] = piece_ref[place]
    copies = []
    for x in range(tiles):
        total = None
        for place_ref, block_ref in zip(places, blocks):
            picked = jnp.concatenate(
                [received[place_ref[x, k]] for k in range(per_block)], axis=1
            )
            part = jnp.dot(
                picked,
                block_ref[x].reshape(per_block * inner, columns),
                preferred_element_type=jnp.float32,
            )
            total = part if total is None else total + part
        stage[x] = total.astype(stage.dtype)
        copy = pltpu.make_async_copy(stage.at[x], out_ref.at[x], sems.at[x])
        copy.start()
        copies.append(copy)
    for copy in copies:
        copy.wait()


def regrouped(arrays, width, count):
    shape = jax.ShapeDtypeStruct((len(arrays) * width,) + arrays[0].shape[1:], arrays[0].dtype)
    return pl.pallas_call(
        functools.partial(regroup, len(arrays), width),
        out_shape=[shape] * count,
        in_specs=[VMEM] * len(arrays),
        out_specs=[VMEM] * count,
        compiler_params=GRANT,
    )(*arrays)


def on_device(wide, narrow, amplitudes, send_list, tile_positions, integrals):
    cap = send_list.shape[1] // wide
    pairs, columns = amplitudes.shape[1:]
    tiles = integrals.shape[0]
    near = math.isqrt(wide)
    far = wide // near
    units = [(slot, part) for slot in range(cap) for part in range(PARTS)]
    early, late = units[:-LATE], units[-LATE:]

    def exchange(array, partner):
        return lax.ppermute(array, "wide", [(d, d ^ partner) for d in range(wide)])

    along = [[(1, a + near * b, s) for a in range(near) for s in early] for b in range(far)]
    everyone = [(0, d, s) for d in range(wide) for s in late]
    plan = along + [everyone]
    outgoing = pl.pallas_call(
        functools.partial(pick_outgoing, plan, cap),
        out_shape=[jax.ShapeDtypeStruct((len(p), pairs // PARTS, columns), amplitudes.dtype) for p in plan],
        in_specs=[ANYWHERE, ANYWHERE],
        out_specs=[VMEM] * len(plan),
        scratch_shapes=[
            pltpu.SMEM(send_list.shape, send_list.dtype),
            pltpu.VMEM(amplitudes.shape, amplitudes.dtype),
            pltpu.SemaphoreType.DMA((2,)),
        ],
        compiler_params=GRANT,
    )(send_list, amplitudes)
    if narrow == 2:
        swap = [(0, 1), (1, 0)]
        places = [tile_positions, lax.ppermute(tile_positions, "narrow", swap)]
        blocks = [integrals, lax.ppermute(integrals, "narrow", swap)]
    else:
        places = [lax.all_gather(tile_positions, "narrow", axis=1, tiled=True)]
        blocks = [lax.all_gather(integrals, "narrow", axis=1, tiled=True)]
    got_along = [outgoing[0]] + [None] * (far - 1)
    for b in range(far - 1, 0, -1):
        got_along[b] = exchange(outgoing[b], near * b)
    direct = lax.all_to_all(outgoing[far], "wide", split_axis=0, concat_axis=0, tiled=True)
    across = regrouped(got_along, len(early), near - 1)
    got_across = [exchange(across[a - 1], a) for a in range(near - 1, 0, -1)]
    pieces = [direct] + got_along[:1] + got_along[:0:-1] + got_across
    origins = [list(enumerate(everyone))]
    origins += [list(enumerate((1, near * b, s) for s in early)) for b in [0, *range(far - 1, 0, -1)]]
    origins += [list(enumerate((1, a + near * b, s) for b in range(far) for s in early)) for a in range(near - 1, 0, -1)]
    count = len(blocks)
    return pl.pallas_call(
        functools.partial(contract, origins, cap, count),
        out_shape=jax.ShapeDtypeStruct((tiles, pairs, columns), jnp.bfloat16),
        in_specs=[SMEM] * count + [VMEM] * (len(pieces) + count),
        out_specs=ANYWHERE,
        scratch_shapes=[
            pltpu.VMEM((cap * wide, pairs, columns), amplitudes.dtype),
            pltpu.VMEM((tiles, pairs, columns), jnp.bfloat16),
            pltpu.SemaphoreType.DMA((tiles,)),
        ],
        compiler_params=GRANT,
    )(*places, *pieces, *blocks)


def solution(mesh):
    placed = (
        P("wide", "narrow", None),
        P("wide", None),
        P("wide", "narrow"),
        P("wide", "narrow", None, None),
    )
    return jax.shard_map(
        functools.partial(on_device, mesh.shape["wide"], mesh.shape["narrow"]),
        mesh=mesh,
        in_specs=placed,
        out_specs=P("wide", "narrow", None),
        check_vma=False,
    )
```

```python
import functools
import math

import jax
import jax.numpy as jnp
from jax import lax
from jax.experimental import pallas as pl
from jax.experimental.pallas import tpu as pltpu
from jax.sharding import PartitionSpec as P

SMEM = pl.BlockSpec(memory_space=pltpu.SMEM)
VMEM = pl.BlockSpec(memory_space=pltpu.VMEM)
ANYWHERE = pl.BlockSpec(memory_space=pl.ANY)


PARTS = 4
LATE = 5
GRANT = pltpu.CompilerParams(vmem_limit_bytes=48 * 1024 * 1024)


def pick_outgoing(plan, cap, send_ref, amplitudes_ref, *refs):
    out_refs = refs[: len(plan)]
    sends, held, sems = refs[len(plan) :]
    fetch_sends = pltpu.make_async_copy(send_ref, sends, sems.at[0])
    fetch_tiles = pltpu.make_async_copy(amplitudes_ref, held, sems.at[1])
    fetch_tiles.start()
    fetch_sends.start()
    fetch_sends.wait()
    fetch_tiles.wait()
    me = lax.axis_index("wide")
    for wanted, out_ref in zip(plan, out_refs):
        rows = out_ref.shape[1]
        for place, (partner, (slot, part)) in enumerate(wanted):
            tile = sends[0, (me ^ partner) * cap + slot]
            out_ref[place] = held[tile, part * rows : (part + 1) * rows]


def regroup(ins, width, staged, *refs):
    in_refs, stage_in = refs[:ins], refs[ins : ins + staged]
    out_refs = refs[ins + staged :]
    copies = []
    if staged:
        out_refs, stage_out, sems = out_refs[: -staged - 1], out_refs[-staged - 1 : -1], out_refs[-1]
        for number in range(staged):
            copy = pltpu.make_async_copy(stage_in[number], stage_out[number], sems.at[number])
            copy.start()
            copies.append(copy)
    for j, out_ref in enumerate(out_refs):
        for i, in_ref in enumerate(in_refs):
            out_ref[i * width : (i + 1) * width] = in_ref[(j + 1) * width : (j + 2) * width]
    for copy in copies:
        copy.wait()


def contract(plan, cap, count, *refs):
    places = refs[:count]
    pieces = refs[count : count + len(plan)]
    blocks = list(refs[count + len(plan) : 2 * count + len(plan)])
    out_ref, received, stage, sems = refs[2 * count + len(plan) :]
    tiles, per_block, inner, columns = blocks[0].shape
    me = lax.axis_index("wide")
    for origin, piece_ref in zip(plan, pieces):
        rows = piece_ref.shape[1]
        for place, (partner, (slot, part)) in origin:
            received[(me ^ partner) * cap + slot, part * rows : (part + 1) * rows] = piece_ref[place]
    copies = []
    for x in range(tiles):
        total = None
        for place_ref, block_ref in zip(places, blocks):
            picked = jnp.concatenate(
                [received[place_ref[x, k]] for k in range(per_block)], axis=1
            )
            part = jnp.dot(
                picked,
                block_ref[x].reshape(per_block * inner, columns),
                preferred_element_type=jnp.float32,
            )
            total = part if total is None else total + part
        stage[x] = total.astype(stage.dtype)
        copy = pltpu.make_async_copy(stage.at[x], out_ref.at[x], sems.at[x])
        copy.start()
        copies.append(copy)
    for copy in copies:
        copy.wait()


def regrouped(arrays, width, count, staged=()):
    shape = jax.ShapeDtypeStruct((len(arrays) * width,) + arrays[0].shape[1:], arrays[0].dtype)
    outs = pl.pallas_call(
        functools.partial(regroup, len(arrays), width, len(staged)),
        out_shape=[shape] * count + [jax.ShapeDtypeStruct(s.shape, s.dtype) for s in staged],
        in_specs=[VMEM] * len(arrays) + [ANYWHERE] * len(staged),
        out_specs=[VMEM] * (count + len(staged)),
        scratch_shapes=[pltpu.SemaphoreType.DMA((len(staged),))] if staged else [],
        compiler_params=GRANT,
    )(*arrays, *staged)
    return list(outs[:count]), list(outs[count:])


def on_device(wide, narrow, amplitudes, send_list, tile_positions, integrals):
    cap = send_list.shape[1] // wide
    pairs, columns = amplitudes.shape[1:]
    tiles = integrals.shape[0]
    near = math.isqrt(wide)
    far = wide // near
    units = [(slot, part) for slot in range(cap) for part in range(PARTS)]
    early, late = units[:-LATE], units[-LATE:]

    def exchange(array, partner):
        return lax.ppermute(array, "wide", [(d, d ^ partner) for d in range(wide)])

    along = [[(a + near * b, s) for a in range(near) for s in early] for b in range(far)]
    across = [[(a + near * b, s) for b in range(far) for s in late] for a in range(near)]
    plan = along + across
    outgoing = pl.pallas_call(
        functools.partial(pick_outgoing, plan, cap),
        out_shape=[jax.ShapeDtypeStruct((len(p), pairs // PARTS, columns), amplitudes.dtype) for p in plan],
        in_specs=[ANYWHERE, ANYWHERE],
        out_specs=[VMEM] * len(plan),
        scratch_shapes=[
            pltpu.SMEM(send_list.shape, send_list.dtype),
            pltpu.VMEM(amplitudes.shape, amplitudes.dtype),
            pltpu.SemaphoreType.DMA((2,)),
        ],
        compiler_params=GRANT,
    )(send_list, amplitudes)
    if narrow == 2:
        swap = [(0, 1), (1, 0)]
        places = [tile_positions, lax.ppermute(tile_positions, "narrow", swap)]
        blocks = [integrals, lax.ppermute(integrals, "narrow", swap)]
    else:
        places = [lax.all_gather(tile_positions, "narrow", axis=1, tiled=True)]
        blocks = [lax.all_gather(integrals, "narrow", axis=1, tiled=True)]
    first_along, first_across = outgoing[:far], outgoing[far:]
    got_across = [first_across[0]] + [None] * (near - 1)
    got_along = [first_along[0]] + [None] * (far - 1)
    for a in range(near - 1, 0, -1):
        got_across[a] = exchange(first_across[a], a)
    for b in range(far - 1, 0, -1):
        got_along[b] = exchange(first_along[b], near * b)
    second_along, _ = regrouped(got_across, len(late), far - 1)
    second_along, blocks[-1] = lax.optimization_barrier((second_along, blocks[-1]))
    got_along[0], second_along[-1] = lax.optimization_barrier((got_along[0], second_along[-1]))
    last_along = [exchange(second_along[b - 1], near * b) for b in range(far - 1, 0, -1)]
    if narrow == 2:
        got_along[0], places[-1] = lax.optimization_barrier((got_along[0], places[-1]))
    sets = [range(far // 2), range(far - 1, far // 2 - 1, -1)]
    last_across = []
    for members in sets:
        staged = (places[0], blocks[0]) if narrow == 2 and members is sets[1] else ()
        second_across, staged = regrouped([got_along[b] for b in members], len(early), near - 1, staged)
        if staged:
            places[0], blocks[0] = staged
        last_across += [exchange(second_across[a - 1], a) for a in range(near - 1, 0, -1)]
    pieces = got_across + got_along[:1] + got_along[:0:-1] + last_along + last_across
    origins = [list(enumerate((a, s) for s in late)) for a in range(near)]
    origins += [list(enumerate((near * b, s) for s in early)) for b in [0, *range(far - 1, 0, -1)]]
    origins += [list(enumerate((a + near * b, s) for a in range(near) for s in late)) for b in range(far - 1, 0, -1)]
    origins += [
        list(enumerate((a + near * b, s) for b in members for s in early))
        for members in sets
        for a in range(near - 1, 0, -1)
    ]
    count = len(blocks)
    return pl.pallas_call(
        functools.partial(contract, origins, cap, count),
        out_shape=jax.ShapeDtypeStruct((tiles, pairs, columns), jnp.bfloat16),
        in_specs=[SMEM] * count + [VMEM] * (len(pieces) + count),
        out_specs=ANYWHERE,
        scratch_shapes=[
            pltpu.VMEM((cap * wide, pairs, columns), amplitudes.dtype),
            pltpu.VMEM((tiles, pairs, columns), jnp.bfloat16),
            pltpu.SemaphoreType.DMA((tiles,)),
        ],
        compiler_params=GRANT,
    )(*places, *pieces, *blocks)


def solution(mesh):
    placed = (
        P("wide", "narrow", None),
        P("wide", None),
        P("wide", "narrow"),
        P("wide", "narrow", None, None),
    )
    return jax.shard_map(
        functools.partial(on_device, mesh.shape["wide"], mesh.shape["narrow"]),
        mesh=mesh,
        in_specs=placed,
        out_specs=P("wide", "narrow", None),
        check_vma=False,
    )
```

```python
import functools
import math

import jax
import jax.numpy as jnp
from jax import lax
from jax.experimental import pallas as pl
from jax.experimental.pallas import tpu as pltpu
from jax.sharding import PartitionSpec as P

SMEM = pl.BlockSpec(memory_space=pltpu.SMEM)
VMEM = pl.BlockSpec(memory_space=pltpu.VMEM)
ANYWHERE = pl.BlockSpec(memory_space=pl.ANY)


GRANT = pltpu.CompilerParams(vmem_limit_bytes=48 * 1024 * 1024)


def pick_outgoing(plan, cap, send_ref, amplitudes_ref, *refs):
    out_refs = refs[: len(plan)]
    sends, held, sems = refs[len(plan) :]
    fetch_sends = pltpu.make_async_copy(send_ref, sends, sems.at[0])
    fetch_tiles = pltpu.make_async_copy(amplitudes_ref, held, sems.at[1])
    fetch_tiles.start()
    fetch_sends.start()
    fetch_sends.wait()
    fetch_tiles.wait()
    me = lax.axis_index("wide")
    for wanted, out_ref in zip(plan, out_refs):
        for place, (partner, slot) in enumerate(wanted):
            out_ref[place] = held[sends[0, (me ^ partner) * cap + slot]]


def regroup(ins, width, staged, *refs):
    in_refs, stage_in = refs[:ins], refs[ins : ins + staged]
    out_refs = refs[ins + staged :]
    copies = []
    if staged:
        out_refs, stage_out, sems = out_refs[: -staged - 1], out_refs[-staged - 1 : -1], out_refs[-1]
        for number in range(staged):
            copy = pltpu.make_async_copy(stage_in[number], stage_out[number], sems.at[number])
            copy.start()
            copies.append(copy)
    for j, out_ref in enumerate(out_refs):
        for i, in_ref in enumerate(in_refs):
            out_ref[i * width : (i + 1) * width] = in_ref[(j + 1) * width : (j + 2) * width]
    for copy in copies:
        copy.wait()


def contract(plan, cap, count, *refs):
    places = refs[:count]
    pieces = refs[count : count + len(plan)]
    blocks = list(refs[count + len(plan) : 2 * count + len(plan)])
    out_ref, received, stage, sems = refs[2 * count + len(plan) :]
    tiles, per_block, inner, columns = blocks[0].shape
    me = lax.axis_index("wide")
    for origin, piece_ref in zip(plan, pieces):
        for place, (partner, slot) in origin:
            received[(me ^ partner) * cap + slot] = piece_ref[place]
    copies = []
    for x in range(tiles):
        total = None
        for place_ref, block_ref in zip(places, blocks):
            picked = jnp.concatenate(
                [received[place_ref[x, k]] for k in range(per_block)], axis=1
            )
            part = jnp.dot(
                picked,
                block_ref[x].reshape(per_block * inner, columns),
                preferred_element_type=jnp.float32,
            )
            total = part if total is None else total + part
        stage[x] = total.astype(stage.dtype)
        copy = pltpu.make_async_copy(stage.at[x], out_ref.at[x], sems.at[x])
        copy.start()
        copies.append(copy)
    for copy in copies:
        copy.wait()


def regrouped(arrays, width, count, staged=()):
    shape = jax.ShapeDtypeStruct((len(arrays) * width,) + arrays[0].shape[1:], arrays[0].dtype)
    outs = pl.pallas_call(
        functools.partial(regroup, len(arrays), width, len(staged)),
        out_shape=[shape] * count + [jax.ShapeDtypeStruct(s.shape, s.dtype) for s in staged],
        in_specs=[VMEM] * len(arrays) + [ANYWHERE] * len(staged),
        out_specs=[VMEM] * (count + len(staged)),
        scratch_shapes=[pltpu.SemaphoreType.DMA((len(staged),))] if staged else [],
        compiler_params=GRANT,
    )(*arrays, *staged)
    return list(outs[:count]), list(outs[count:])


def on_device(wide, narrow, amplitudes, send_list, tile_positions, integrals):
    cap = send_list.shape[1] // wide
    pairs, columns = amplitudes.shape[1:]
    tiles = integrals.shape[0]
    near = math.isqrt(wide)
    far = wide // near
    early, late = range(cap // 2), range(cap // 2, cap)

    def exchange(array, partner):
        return lax.ppermute(array, "wide", [(d, d ^ partner) for d in range(wide)])

    along = [[(a + near * b, s) for a in range(near) for s in early] for b in range(far)]
    across = [[(a + near * b, s) for b in range(far) for s in late] for a in range(near)]
    plan = along + across
    outgoing = pl.pallas_call(
        functools.partial(pick_outgoing, plan, cap),
        out_shape=[jax.ShapeDtypeStruct((len(p), pairs, columns), amplitudes.dtype) for p in plan],
        in_specs=[ANYWHERE, ANYWHERE],
        out_specs=[VMEM] * len(plan),
        scratch_shapes=[
            pltpu.SMEM(send_list.shape, send_list.dtype),
            pltpu.VMEM(amplitudes.shape, amplitudes.dtype),
            pltpu.SemaphoreType.DMA((2,)),
        ],
        compiler_params=GRANT,
    )(send_list, amplitudes)
    if narrow == 2:
        swap = [(0, 1), (1, 0)]
        places = [tile_positions, lax.ppermute(tile_positions, "narrow", swap)]
        blocks = [integrals, lax.ppermute(integrals, "narrow", swap)]
    else:
        places = [lax.all_gather(tile_positions, "narrow", axis=1, tiled=True)]
        blocks = [lax.all_gather(integrals, "narrow", axis=1, tiled=True)]
    first_along, first_across = outgoing[:far], outgoing[far:]
    got_across = [first_across[0]] + [None] * (near - 1)
    got_along = [first_along[0]] + [None] * (far - 1)
    for a in range(near - 1, 0, -1):
        got_across[a] = exchange(first_across[a], a)
    for b in range(far - 1, 0, -1):
        got_along[b] = exchange(first_along[b], near * b)
    second_along, kept = regrouped(got_across, len(late), far - 1, (places[0], blocks[0]) if narrow == 2 else ())
    if narrow == 2:
        places[0], blocks[0] = kept
    second_along, blocks[-1] = lax.optimization_barrier((second_along, blocks[-1]))
    got_along[0], second_along[-1] = lax.optimization_barrier((got_along[0], second_along[-1]))
    last_along = [exchange(second_along[b - 1], near * b) for b in range(far - 1, 0, -1)]
    got_along[0], places[-1] = lax.optimization_barrier((got_along[0], places[-1]))
    second_across, _ = regrouped(got_along, len(early), near - 1)
    last_across = [exchange(second_across[a - 1], a) for a in range(near - 1, 0, -1)]
    pieces = got_across + got_along[:1] + got_along[:0:-1] + last_along + last_across
    origins = [list(enumerate((a, s) for s in late)) for a in range(near)]
    origins += [list(enumerate((near * b, s) for s in early)) for b in [0, *range(far - 1, 0, -1)]]
    origins += [list(enumerate((a + near * b, s) for a in range(near) for s in late)) for b in range(far - 1, 0, -1)]
    origins += [list(enumerate((a + near * b, s) for b in range(far) for s in early)) for a in range(near - 1, 0, -1)]
    count = len(blocks)
    return pl.pallas_call(
        functools.partial(contract, origins, cap, count),
        out_shape=jax.ShapeDtypeStruct((tiles, pairs, columns), jnp.bfloat16),
        in_specs=[SMEM] * count + [VMEM] * (len(pieces) + count),
        out_specs=ANYWHERE,
        scratch_shapes=[
            pltpu.VMEM((cap * wide, pairs, columns), amplitudes.dtype),
            pltpu.VMEM((tiles, pairs, columns), jnp.bfloat16),
            pltpu.SemaphoreType.DMA((tiles,)),
        ],
        compiler_params=GRANT,
    )(*places, *pieces, *blocks)


def solution(mesh):
    placed = (
        P("wide", "narrow", None),
        P("wide", None),
        P("wide", "narrow"),
        P("wide", "narrow", None, None),
    )
    return jax.shard_map(
        functools.partial(on_device, mesh.shape["wide"], mesh.shape["narrow"]),
        mesh=mesh,
        in_specs=placed,
        out_specs=P("wide", "narrow", None),
        check_vma=False,
    )
```

```python
import functools
import math

import jax
import jax.numpy as jnp
from jax import lax
from jax.experimental import pallas as pl
from jax.experimental.pallas import tpu as pltpu
from jax.sharding import PartitionSpec as P

SMEM = pl.BlockSpec(memory_space=pltpu.SMEM)
VMEM = pl.BlockSpec(memory_space=pltpu.VMEM)
ANYWHERE = pl.BlockSpec(memory_space=pl.ANY)


GRANT = pltpu.CompilerParams(vmem_limit_bytes=48 * 1024 * 1024)


def pick_outgoing(plan, cap, send_ref, amplitudes_ref, *refs):
    out_refs = refs[: len(plan)]
    sends, held, sems = refs[len(plan) :]
    fetch_sends = pltpu.make_async_copy(send_ref, sends, sems.at[0])
    fetch_tiles = pltpu.make_async_copy(amplitudes_ref, held, sems.at[1])
    fetch_tiles.start()
    fetch_sends.start()
    fetch_sends.wait()
    fetch_tiles.wait()
    me = lax.axis_index("wide")
    for wanted, out_ref in zip(plan, out_refs):
        for place, (partner, slot) in enumerate(wanted):
            out_ref[place] = held[sends[0, (me ^ partner) * cap + slot]]


def regroup(ins, width, staged, *refs):
    in_refs, stage_in = refs[:ins], refs[ins : ins + staged]
    out_refs = refs[ins + staged :]
    copies = []
    if staged:
        out_refs, stage_out, sems = out_refs[: -staged - 1], out_refs[-staged - 1 : -1], out_refs[-1]
        for number in range(staged):
            copy = pltpu.make_async_copy(stage_in[number], stage_out[number], sems.at[number])
            copy.start()
            copies.append(copy)
    for j, out_ref in enumerate(out_refs):
        for i, in_ref in enumerate(in_refs):
            out_ref[i * width : (i + 1) * width] = in_ref[(j + 1) * width : (j + 2) * width]
    for copy in copies:
        copy.wait()


def contract(plan, cap, count, *refs):
    places = refs[:count]
    pieces = refs[count : count + len(plan)]
    blocks = list(refs[count + len(plan) : 2 * count + len(plan)])
    out_ref, received, stage, sems = refs[2 * count + len(plan) :]
    tiles, per_block, inner, columns = blocks[0].shape
    me = lax.axis_index("wide")
    for origin, piece_ref in zip(plan, pieces):
        for place, (partner, slot) in origin:
            received[(me ^ partner) * cap + slot] = piece_ref[place]
    copies = []
    for x in range(tiles):
        total = None
        for place_ref, block_ref in zip(places, blocks):
            picked = jnp.concatenate(
                [received[place_ref[x, k]] for k in range(per_block)], axis=1
            )
            part = jnp.dot(
                picked,
                block_ref[x].reshape(per_block * inner, columns),
                preferred_element_type=jnp.float32,
            )
            total = part if total is None else total + part
        stage[x] = total.astype(stage.dtype)
        copy = pltpu.make_async_copy(stage.at[x], out_ref.at[x], sems.at[x])
        copy.start()
        copies.append(copy)
    for copy in copies:
        copy.wait()


def regrouped(arrays, width, count, staged=()):
    shape = jax.ShapeDtypeStruct((len(arrays) * width,) + arrays[0].shape[1:], arrays[0].dtype)
    outs = pl.pallas_call(
        functools.partial(regroup, len(arrays), width, len(staged)),
        out_shape=[shape] * count + [jax.ShapeDtypeStruct(s.shape, s.dtype) for s in staged],
        in_specs=[VMEM] * len(arrays) + [ANYWHERE] * len(staged),
        out_specs=[VMEM] * (count + len(staged)),
        scratch_shapes=[pltpu.SemaphoreType.DMA((len(staged),))] if staged else [],
        compiler_params=GRANT,
    )(*arrays, *staged)
    return list(outs[:count]), list(outs[count:])


def on_device(wide, narrow, amplitudes, send_list, tile_positions, integrals):
    cap = send_list.shape[1] // wide
    pairs, columns = amplitudes.shape[1:]
    tiles = integrals.shape[0]
    near = math.isqrt(wide)
    far = wide // near
    early, late = range(cap // 2), range(cap // 2, cap)

    def exchange(array, partner):
        return lax.ppermute(array, "wide", [(d, d ^ partner) for d in range(wide)])

    along = [[(a + near * b, s) for a in range(near) for s in early] for b in range(far)]
    across = [[(a + near * b, s) for b in range(far) for s in late] for a in range(near)]
    plan = along + across
    outgoing = pl.pallas_call(
        functools.partial(pick_outgoing, plan, cap),
        out_shape=[jax.ShapeDtypeStruct((len(p), pairs, columns), amplitudes.dtype) for p in plan],
        in_specs=[ANYWHERE, ANYWHERE],
        out_specs=[VMEM] * len(plan),
        scratch_shapes=[
            pltpu.SMEM(send_list.shape, send_list.dtype),
            pltpu.VMEM(amplitudes.shape, amplitudes.dtype),
            pltpu.SemaphoreType.DMA((2,)),
        ],
        compiler_params=GRANT,
    )(send_list, amplitudes)
    if narrow == 2:
        swap = [(0, 1), (1, 0)]
        places = [tile_positions, lax.ppermute(tile_positions, "narrow", swap)]
        blocks = [integrals, lax.ppermute(integrals, "narrow", swap)]
    else:
        places = [lax.all_gather(tile_positions, "narrow", axis=1, tiled=True)]
        blocks = [lax.all_gather(integrals, "narrow", axis=1, tiled=True)]
    first_along, first_across = list(outgoing[:far]), outgoing[far:]
    got_across = [first_across[0]] + [None] * (near - 1)
    got_along = [first_along[0]] + [None] * (far - 1)
    for a in range(near - 1, 0, -1):
        got_across[a] = exchange(first_across[a], a)
    for b in range(far - 1, 0, -1):
        if b == far // 2:
            first_along[b], blocks[-1] = lax.optimization_barrier((first_along[b], blocks[-1]))
        got_along[b] = exchange(first_along[b], near * b)
    second_along, kept = regrouped(got_across, len(late), far - 1, (places[0], blocks[0]) if narrow == 2 else ())
    if narrow == 2:
        places[0], blocks[0] = kept
    got_along[0], second_along[-1] = lax.optimization_barrier((got_along[0], second_along[-1]))
    middle = far // 2
    got_along[middle], second_along[middle - 1] = lax.optimization_barrier(
        (got_along[middle], second_along[middle - 1])
    )
    last_along = [exchange(second_along[b - 1], near * b) for b in range(far - 1, 0, -1)]
    got_along[0], places[-1] = lax.optimization_barrier((got_along[0], places[-1]))
    second_across, _ = regrouped(got_along, len(early), near - 1)
    last_across = [exchange(second_across[a - 1], a) for a in range(near - 1, 0, -1)]
    pieces = got_across + got_along[:1] + got_along[:0:-1] + last_along + last_across
    origins = [list(enumerate((a, s) for s in late)) for a in range(near)]
    origins += [list(enumerate((near * b, s) for s in early)) for b in [0, *range(far - 1, 0, -1)]]
    origins += [list(enumerate((a + near * b, s) for a in range(near) for s in late)) for b in range(far - 1, 0, -1)]
    origins += [list(enumerate((a + near * b, s) for b in range(far) for s in early)) for a in range(near - 1, 0, -1)]
    count = len(blocks)
    return pl.pallas_call(
        functools.partial(contract, origins, cap, count),
        out_shape=jax.ShapeDtypeStruct((tiles, pairs, columns), jnp.bfloat16),
        in_specs=[SMEM] * count + [VMEM] * (len(pieces) + count),
        out_specs=ANYWHERE,
        scratch_shapes=[
            pltpu.VMEM((cap * wide, pairs, columns), amplitudes.dtype),
            pltpu.VMEM((tiles, pairs, columns), jnp.bfloat16),
            pltpu.SemaphoreType.DMA((tiles,)),
        ],
        compiler_params=GRANT,
    )(*places, *pieces, *blocks)


def solution(mesh):
    placed = (
        P("wide", "narrow", None),
        P("wide", None),
        P("wide", "narrow"),
        P("wide", "narrow", None, None),
    )
    return jax.shard_map(
        functools.partial(on_device, mesh.shape["wide"], mesh.shape["narrow"]),
        mesh=mesh,
        in_specs=placed,
        out_specs=P("wide", "narrow", None),
        check_vma=False,
    )
```

```python
import functools
import math

import jax
import jax.numpy as jnp
from jax import lax
from jax.experimental import pallas as pl
from jax.experimental.pallas import tpu as pltpu
from jax.sharding import PartitionSpec as P

SMEM = pl.BlockSpec(memory_space=pltpu.SMEM)
VMEM = pl.BlockSpec(memory_space=pltpu.VMEM)
ANYWHERE = pl.BlockSpec(memory_space=pl.ANY)


GRANT = pltpu.CompilerParams(vmem_limit_bytes=48 * 1024 * 1024)


def pick_outgoing(plan, cap, send_ref, amplitudes_ref, *refs):
    out_refs = refs[: len(plan)]
    sends, held, sems = refs[len(plan) :]
    fetch_sends = pltpu.make_async_copy(send_ref, sends, sems.at[0])
    fetch_tiles = pltpu.make_async_copy(amplitudes_ref, held, sems.at[1])
    fetch_tiles.start()
    fetch_sends.start()
    fetch_sends.wait()
    fetch_tiles.wait()
    me = lax.axis_index("wide")
    for wanted, out_ref in zip(plan, out_refs):
        for place, (partner, slot) in enumerate(wanted):
            out_ref[place] = held[sends[0, (me ^ partner) * cap + slot]]


def regroup(ins, width, staged, *refs):
    in_refs, stage_in = refs[:ins], refs[ins : ins + staged]
    out_refs = refs[ins + staged :]
    copies = []
    if staged:
        out_refs, stage_out, sems = out_refs[: -staged - 1], out_refs[-staged - 1 : -1], out_refs[-1]
        for number in range(staged):
            copy = pltpu.make_async_copy(stage_in[number], stage_out[number], sems.at[number])
            copy.start()
            copies.append(copy)
    for j, out_ref in enumerate(out_refs):
        for i, in_ref in enumerate(in_refs):
            out_ref[i * width : (i + 1) * width] = in_ref[(j + 1) * width : (j + 2) * width]
    for copy in copies:
        copy.wait()


def contract(plan, cap, count, *refs):
    places = refs[:count]
    pieces = refs[count : count + len(plan)]
    blocks = list(refs[count + len(plan) : 2 * count + len(plan)])
    out_ref, received, stage, sems = refs[2 * count + len(plan) :]
    tiles, per_block, inner, columns = blocks[0].shape
    me = lax.axis_index("wide")
    for origin, piece_ref in zip(plan, pieces):
        for place, (partner, slot) in origin:
            received[(me ^ partner) * cap + slot] = piece_ref[place]
    copies = []
    for x in range(tiles):
        total = None
        for place_ref, block_ref in zip(places, blocks):
            picked = jnp.concatenate(
                [received[place_ref[x, k]] for k in range(per_block)], axis=1
            )
            part = jnp.dot(
                picked,
                block_ref[x].reshape(per_block * inner, columns),
                preferred_element_type=jnp.float32,
            )
            total = part if total is None else total + part
        stage[x] = total.astype(stage.dtype)
        copy = pltpu.make_async_copy(stage.at[x], out_ref.at[x], sems.at[x])
        copy.start()
        copies.append(copy)
    for copy in copies:
        copy.wait()


def regrouped(arrays, width, count, staged=()):
    shape = jax.ShapeDtypeStruct((len(arrays) * width,) + arrays[0].shape[1:], arrays[0].dtype)
    outs = pl.pallas_call(
        functools.partial(regroup, len(arrays), width, len(staged)),
        out_shape=[shape] * count + [jax.ShapeDtypeStruct(s.shape, s.dtype) for s in staged],
        in_specs=[VMEM] * len(arrays) + [ANYWHERE] * len(staged),
        out_specs=[VMEM] * (count + len(staged)),
        scratch_shapes=[pltpu.SemaphoreType.DMA((len(staged),))] if staged else [],
        compiler_params=GRANT,
    )(*arrays, *staged)
    return list(outs[:count]), list(outs[count:])


def on_device(wide, narrow, amplitudes, send_list, tile_positions, integrals):
    cap = send_list.shape[1] // wide
    pairs, columns = amplitudes.shape[1:]
    tiles = integrals.shape[0]
    near = math.isqrt(wide)
    far = wide // near
    early, late = range(cap // 2), range(cap // 2, cap)

    def exchange(array, partner):
        return lax.ppermute(array, "wide", [(d, d ^ partner) for d in range(wide)])

    along = [[(a + near * b, s) for a in range(near) for s in early] for b in range(far)]
    across = [[(a + near * b, s) for b in range(far) for s in late] for a in range(near)]
    plan = along + across
    outgoing = pl.pallas_call(
        functools.partial(pick_outgoing, plan, cap),
        out_shape=[jax.ShapeDtypeStruct((len(p), pairs, columns), amplitudes.dtype) for p in plan],
        in_specs=[ANYWHERE, ANYWHERE],
        out_specs=[VMEM] * len(plan),
        scratch_shapes=[
            pltpu.SMEM(send_list.shape, send_list.dtype),
            pltpu.VMEM(amplitudes.shape, amplitudes.dtype),
            pltpu.SemaphoreType.DMA((2,)),
        ],
        compiler_params=GRANT,
    )(send_list, amplitudes)
    if narrow == 2:
        swap = [(0, 1), (1, 0)]
        places = [tile_positions, lax.ppermute(tile_positions, "narrow", swap)]
        blocks = [integrals, lax.ppermute(integrals, "narrow", swap)]
    else:
        places = [lax.all_gather(tile_positions, "narrow", axis=1, tiled=True)]
        blocks = [lax.all_gather(integrals, "narrow", axis=1, tiled=True)]
    first_along, first_across = list(outgoing[:far]), outgoing[far:]
    got_across = [first_across[0]] + [None] * (near - 1)
    got_along = [first_along[0]] + [None] * (far - 1)
    for a in range(near - 1, 0, -1):
        got_across[a] = exchange(first_across[a], a)
    for b in range(far - 1, 0, -1):
        if b == far // 2:
            first_along[b], blocks[-1] = lax.optimization_barrier((first_along[b], blocks[-1]))
        got_along[b] = exchange(first_along[b], near * b)
    second_along, kept = regrouped(got_across, len(late), far - 1, (places[0], blocks[0]) if narrow == 2 else ())
    if narrow == 2:
        places[0], blocks[0] = kept
    got_along[0], second_along[-1] = lax.optimization_barrier((got_along[0], second_along[-1]))
    middle = far // 2
    got_along[middle], second_along[0] = lax.optimization_barrier((got_along[middle], second_along[0]))
    last_along = [exchange(second_along[b - 1], near * b) for b in range(far - 1, 0, -1)]
    got_along[0], places[-1] = lax.optimization_barrier((got_along[0], places[-1]))
    second_across, _ = regrouped(got_along, len(early), near - 1)
    last_across = [exchange(second_across[a - 1], a) for a in range(near - 1, 0, -1)]
    pieces = got_across + got_along[:1] + got_along[:0:-1] + last_along + last_across
    origins = [list(enumerate((a, s) for s in late)) for a in range(near)]
    origins += [list(enumerate((near * b, s) for s in early)) for b in [0, *range(far - 1, 0, -1)]]
    origins += [list(enumerate((a + near * b, s) for a in range(near) for s in late)) for b in range(far - 1, 0, -1)]
    origins += [list(enumerate((a + near * b, s) for b in range(far) for s in early)) for a in range(near - 1, 0, -1)]
    count = len(blocks)
    return pl.pallas_call(
        functools.partial(contract, origins, cap, count),
        out_shape=jax.ShapeDtypeStruct((tiles, pairs, columns), jnp.bfloat16),
        in_specs=[SMEM] * count + [VMEM] * (len(pieces) + count),
        out_specs=ANYWHERE,
        scratch_shapes=[
            pltpu.VMEM((cap * wide, pairs, columns), amplitudes.dtype),
            pltpu.VMEM((tiles, pairs, columns), jnp.bfloat16),
            pltpu.SemaphoreType.DMA((tiles,)),
        ],
        compiler_params=GRANT,
    )(*places, *pieces, *blocks)


def solution(mesh):
    placed = (
        P("wide", "narrow", None),
        P("wide", None),
        P("wide", "narrow"),
        P("wide", "narrow", None, None),
    )
    return jax.shard_map(
        functools.partial(on_device, mesh.shape["wide"], mesh.shape["narrow"]),
        mesh=mesh,
        in_specs=placed,
        out_specs=P("wide", "narrow", None),
        check_vma=False,
    )
```

```python
import functools
import math

import jax
import jax.numpy as jnp
from jax import lax
from jax.experimental import pallas as pl
from jax.experimental.pallas import tpu as pltpu
from jax.sharding import PartitionSpec as P

SMEM = pl.BlockSpec(memory_space=pltpu.SMEM)
VMEM = pl.BlockSpec(memory_space=pltpu.VMEM)
ANYWHERE = pl.BlockSpec(memory_space=pl.ANY)


GRANT = pltpu.CompilerParams(vmem_limit_bytes=48 * 1024 * 1024)


def pick_outgoing(plan, cap, send_ref, amplitudes_ref, *refs):
    out_refs = refs[: len(plan)]
    sends, held, sems = refs[len(plan) :]
    fetch_sends = pltpu.make_async_copy(send_ref, sends, sems.at[0])
    fetch_tiles = pltpu.make_async_copy(amplitudes_ref, held, sems.at[1])
    fetch_tiles.start()
    fetch_sends.start()
    fetch_sends.wait()
    fetch_tiles.wait()
    me = lax.axis_index("wide")
    for wanted, out_ref in zip(plan, out_refs):
        for place, (partner, slot) in enumerate(wanted):
            out_ref[place] = held[sends[0, (me ^ partner) * cap + slot]]


def regroup(ins, width, staged, *refs):
    in_refs, stage_in = refs[:ins], refs[ins : ins + staged]
    out_refs = refs[ins + staged :]
    copies = []
    if staged:
        out_refs, stage_out, sems = out_refs[: -staged - 1], out_refs[-staged - 1 : -1], out_refs[-1]
        for number in range(staged):
            copy = pltpu.make_async_copy(stage_in[number], stage_out[number], sems.at[number])
            copy.start()
            copies.append(copy)
    for j, out_ref in enumerate(out_refs):
        for i, in_ref in enumerate(in_refs):
            out_ref[i * width : (i + 1) * width] = in_ref[(j + 1) * width : (j + 2) * width]
    for copy in copies:
        copy.wait()


def contract(plan, cap, count, *refs):
    places = refs[:count]
    pieces = refs[count : count + len(plan)]
    blocks = list(refs[count + len(plan) : 2 * count + len(plan)])
    out_ref, received, stage, sems = refs[2 * count + len(plan) :]
    tiles, per_block, inner, columns = blocks[0].shape
    me = lax.axis_index("wide")
    for origin, piece_ref in zip(plan, pieces):
        for place, (partner, slot) in origin:
            received[(me ^ partner) * cap + slot] = piece_ref[place]
    copies = []
    for x in range(tiles):
        total = None
        for place_ref, block_ref in zip(places, blocks):
            picked = jnp.concatenate(
                [received[place_ref[x, k]] for k in range(per_block)], axis=1
            )
            part = jnp.dot(
                picked,
                block_ref[x].reshape(per_block * inner, columns),
                preferred_element_type=jnp.float32,
            )
            total = part if total is None else total + part
        stage[x] = total.astype(stage.dtype)
        copy = pltpu.make_async_copy(stage.at[x], out_ref.at[x], sems.at[x])
        copy.start()
        copies.append(copy)
    for copy in copies:
        copy.wait()


def regrouped(arrays, width, count, staged=()):
    shape = jax.ShapeDtypeStruct((len(arrays) * width,) + arrays[0].shape[1:], arrays[0].dtype)
    outs = pl.pallas_call(
        functools.partial(regroup, len(arrays), width, len(staged)),
        out_shape=[shape] * count + [jax.ShapeDtypeStruct(s.shape, s.dtype) for s in staged],
        in_specs=[VMEM] * len(arrays) + [ANYWHERE] * len(staged),
        out_specs=[VMEM] * (count + len(staged)),
        scratch_shapes=[pltpu.SemaphoreType.DMA((len(staged),))] if staged else [],
        compiler_params=GRANT,
    )(*arrays, *staged)
    return list(outs[:count]), list(outs[count:])


def copy_all(*refs):
    half = len(refs) // 2
    copies = [pltpu.make_async_copy(refs[i], refs[half + i], refs[-1].at[i]) for i in range(half)]
    for copy in copies:
        copy.start()
    for copy in copies:
        copy.wait()


def staged_copy(*arrays):
    return pl.pallas_call(
        copy_all,
        out_shape=[jax.ShapeDtypeStruct(a.shape, a.dtype) for a in arrays],
        in_specs=[ANYWHERE] * len(arrays),
        out_specs=[VMEM] * len(arrays),
        scratch_shapes=[pltpu.SemaphoreType.DMA((len(arrays),))],
        compiler_params=GRANT,
    )(*arrays)


def on_device(wide, narrow, amplitudes, send_list, tile_positions, integrals):
    cap = send_list.shape[1] // wide
    pairs, columns = amplitudes.shape[1:]
    tiles = integrals.shape[0]
    near = math.isqrt(wide)
    far = wide // near
    early, late = range(cap // 2), range(cap // 2, cap)

    def exchange(array, partner):
        return lax.ppermute(array, "wide", [(d, d ^ partner) for d in range(wide)])

    along = [[(a + near * b, s) for a in range(near) for s in early] for b in range(far)]
    across = [[(a + near * b, s) for b in range(far) for s in late] for a in range(near)]
    plan = along + across
    outgoing = pl.pallas_call(
        functools.partial(pick_outgoing, plan, cap),
        out_shape=[jax.ShapeDtypeStruct((len(p), pairs, columns), amplitudes.dtype) for p in plan],
        in_specs=[ANYWHERE, ANYWHERE],
        out_specs=[VMEM] * len(plan),
        scratch_shapes=[
            pltpu.SMEM(send_list.shape, send_list.dtype),
            pltpu.VMEM(amplitudes.shape, amplitudes.dtype),
            pltpu.SemaphoreType.DMA((2,)),
        ],
        compiler_params=GRANT,
    )(send_list, amplitudes)
    if narrow == 2:
        swap = [(0, 1), (1, 0)]
        places = [tile_positions, lax.ppermute(tile_positions, "narrow", swap)]
        blocks = [integrals, lax.ppermute(integrals, "narrow", swap)]
    else:
        places = [lax.all_gather(tile_positions, "narrow", axis=1, tiled=True)]
        blocks = [lax.all_gather(integrals, "narrow", axis=1, tiled=True)]
    first_along, first_across = list(outgoing[:far]), outgoing[far:]
    got_across = [first_across[0]] + [None] * (near - 1)
    got_along = [first_along[0]] + [None] * (far - 1)
    for a in range(near - 1, 0, -1):
        got_across[a] = exchange(first_across[a], a)
    for b in range(far - 1, 0, -1):
        if b == far // 2:
            first_along[b], blocks[-1] = lax.optimization_barrier((first_along[b], blocks[-1]))
        got_along[b] = exchange(first_along[b], near * b)
    second_along, _ = regrouped(got_across, len(late), far - 1)
    got_along[0], second_along[-1] = lax.optimization_barrier((got_along[0], second_along[-1]))
    middle = far // 2
    got_along[middle], second_along[middle - 1] = lax.optimization_barrier(
        (got_along[middle], second_along[middle - 1])
    )
    last_along = [exchange(second_along[b - 1], near * b) for b in range(far - 1, 0, -1)]
    got_along[0], places[-1] = lax.optimization_barrier((got_along[0], places[-1]))
    if narrow == 2:
        source, got_along[middle] = lax.optimization_barrier((blocks[0], got_along[middle]))
        places[0], blocks[0] = staged_copy(places[0], source)
        got_along[0], blocks[0] = lax.optimization_barrier((got_along[0], blocks[0]))
    second_across, _ = regrouped(got_along, len(early), near - 1)
    last_across = [exchange(second_across[a - 1], a) for a in range(near - 1, 0, -1)]
    pieces = got_across + got_along[:1] + got_along[:0:-1] + last_along + last_across
    origins = [list(enumerate((a, s) for s in late)) for a in range(near)]
    origins += [list(enumerate((near * b, s) for s in early)) for b in [0, *range(far - 1, 0, -1)]]
    origins += [list(enumerate((a + near * b, s) for a in range(near) for s in late)) for b in range(far - 1, 0, -1)]
    origins += [list(enumerate((a + near * b, s) for b in range(far) for s in early)) for a in range(near - 1, 0, -1)]
    count = len(blocks)
    return pl.pallas_call(
        functools.partial(contract, origins, cap, count),
        out_shape=jax.ShapeDtypeStruct((tiles, pairs, columns), jnp.bfloat16),
        in_specs=[SMEM] * count + [VMEM] * (len(pieces) + count),
        out_specs=ANYWHERE,
        scratch_shapes=[
            pltpu.VMEM((cap * wide, pairs, columns), amplitudes.dtype),
            pltpu.VMEM((tiles, pairs, columns), jnp.bfloat16),
            pltpu.SemaphoreType.DMA((tiles,)),
        ],
        compiler_params=GRANT,
    )(*places, *pieces, *blocks)


def solution(mesh):
    placed = (
        P("wide", "narrow", None),
        P("wide", None),
        P("wide", "narrow"),
        P("wide", "narrow", None, None),
    )
    return jax.shard_map(
        functools.partial(on_device, mesh.shape["wide"], mesh.shape["narrow"]),
        mesh=mesh,
        in_specs=placed,
        out_specs=P("wide", "narrow", None),
        check_vma=False,
    )
```

```python
import functools
import math

import jax
import jax.numpy as jnp
from jax import lax
from jax.experimental import pallas as pl
from jax.experimental.pallas import tpu as pltpu
from jax.sharding import PartitionSpec as P

SMEM = pl.BlockSpec(memory_space=pltpu.SMEM)
VMEM = pl.BlockSpec(memory_space=pltpu.VMEM)
ANYWHERE = pl.BlockSpec(memory_space=pl.ANY)


GRANT = pltpu.CompilerParams(vmem_limit_bytes=48 * 1024 * 1024)


def pick_outgoing(plan, cap, send_ref, amplitudes_ref, *refs):
    out_refs = refs[: len(plan)]
    sends, sem = refs[len(plan) :]
    fetch_sends = pltpu.make_async_copy(send_ref, sends, sem)
    fetch_sends.start()
    fetch_sends.wait()
    me = lax.axis_index("wide")
    for wanted, out_ref in zip(plan, out_refs):
        for place, (partner, slot) in enumerate(wanted):
            out_ref[place] = amplitudes_ref[sends[0, (me ^ partner) * cap + slot]]


def regroup(ins, width, staged, *refs):
    in_refs, stage_in = refs[:ins], refs[ins : ins + staged]
    out_refs = refs[ins + staged :]
    copies = []
    if staged:
        out_refs, stage_out, sems = out_refs[: -staged - 1], out_refs[-staged - 1 : -1], out_refs[-1]
        for number in range(staged):
            copy = pltpu.make_async_copy(stage_in[number], stage_out[number], sems.at[number])
            copy.start()
            copies.append(copy)
    for j, out_ref in enumerate(out_refs):
        for i, in_ref in enumerate(in_refs):
            out_ref[i * width : (i + 1) * width] = in_ref[(j + 1) * width : (j + 2) * width]
    for copy in copies:
        copy.wait()


def contract(plan, cap, count, *refs):
    places = refs[:count]
    pieces = refs[count : count + len(plan)]
    blocks = list(refs[count + len(plan) : 2 * count + len(plan)])
    out_ref, received, stage, sems = refs[2 * count + len(plan) :]
    tiles, per_block, inner, columns = blocks[0].shape
    me = lax.axis_index("wide")
    for origin, piece_ref in zip(plan, pieces):
        for place, (partner, slot) in origin:
            received[(me ^ partner) * cap + slot] = piece_ref[place]
    copies = []
    for x in range(tiles):
        total = None
        for place_ref, block_ref in zip(places, blocks):
            picked = jnp.concatenate(
                [received[place_ref[x, k]] for k in range(per_block)], axis=1
            )
            part = jnp.dot(
                picked,
                block_ref[x].reshape(per_block * inner, columns),
                preferred_element_type=jnp.float32,
            )
            total = part if total is None else total + part
        stage[x] = total.astype(stage.dtype)
        copy = pltpu.make_async_copy(stage.at[x], out_ref.at[x], sems.at[x])
        copy.start()
        copies.append(copy)
    for copy in copies:
        copy.wait()


def regrouped(arrays, width, count, staged=()):
    shape = jax.ShapeDtypeStruct((len(arrays) * width,) + arrays[0].shape[1:], arrays[0].dtype)
    outs = pl.pallas_call(
        functools.partial(regroup, len(arrays), width, len(staged)),
        out_shape=[shape] * count + [jax.ShapeDtypeStruct(s.shape, s.dtype) for s in staged],
        in_specs=[VMEM] * len(arrays) + [ANYWHERE] * len(staged),
        out_specs=[VMEM] * (count + len(staged)),
        scratch_shapes=[pltpu.SemaphoreType.DMA((len(staged),))] if staged else [],
        compiler_params=GRANT,
    )(*arrays, *staged)
    return list(outs[:count]), list(outs[count:])


def on_device(wide, narrow, amplitudes, send_list, tile_positions, integrals):
    cap = send_list.shape[1] // wide
    pairs, columns = amplitudes.shape[1:]
    tiles = integrals.shape[0]
    near = math.isqrt(wide)
    far = wide // near
    early, late = range(cap // 2), range(cap // 2, cap)

    def exchange(array, partner):
        return lax.ppermute(array, "wide", [(d, d ^ partner) for d in range(wide)])

    along = [[(a + near * b, s) for a in range(near) for s in early] for b in range(far)]
    across = [[(a + near * b, s) for b in range(far) for s in late] for a in range(near)]
    plan = along + across
    outgoing = pl.pallas_call(
        functools.partial(pick_outgoing, plan, cap),
        out_shape=[jax.ShapeDtypeStruct((len(p), pairs, columns), amplitudes.dtype) for p in plan],
        in_specs=[ANYWHERE, VMEM],
        out_specs=[VMEM] * len(plan),
        scratch_shapes=[
            pltpu.SMEM(send_list.shape, send_list.dtype),
            pltpu.SemaphoreType.DMA,
        ],
        compiler_params=GRANT,
    )(send_list, amplitudes)
    if narrow == 2:
        swap = [(0, 1), (1, 0)]
        places = [tile_positions, lax.ppermute(tile_positions, "narrow", swap)]
        blocks = [integrals, lax.ppermute(integrals, "narrow", swap)]
    else:
        places = [lax.all_gather(tile_positions, "narrow", axis=1, tiled=True)]
        blocks = [lax.all_gather(integrals, "narrow", axis=1, tiled=True)]
    first_along, first_across = list(outgoing[:far]), outgoing[far:]
    got_across = [first_across[0]] + [None] * (near - 1)
    got_along = [first_along[0]] + [None] * (far - 1)
    for a in range(near - 1, 0, -1):
        got_across[a] = exchange(first_across[a], a)
    for b in range(far - 1, 0, -1):
        if b == far // 2:
            first_along[b], blocks[-1] = lax.optimization_barrier((first_along[b], blocks[-1]))
        got_along[b] = exchange(first_along[b], near * b)
    second_along, kept = regrouped(got_across, len(late), far - 1, (places[0], blocks[0]) if narrow == 2 else ())
    if narrow == 2:
        places[0], blocks[0] = kept
    got_along[0], second_along[-1] = lax.optimization_barrier((got_along[0], second_along[-1]))
    middle = far // 2
    got_along[middle], second_along[middle - 1] = lax.optimization_barrier(
        (got_along[middle], second_along[middle - 1])
    )
    last_along = [exchange(second_along[b - 1], near * b) for b in range(far - 1, 0, -1)]
    got_along[0], places[-1] = lax.optimization_barrier((got_along[0], places[-1]))
    second_across, _ = regrouped(got_along, len(early), near - 1)
    last_across = [exchange(second_across[a - 1], a) for a in range(near - 1, 0, -1)]
    pieces = got_across + got_along[:1] + got_along[:0:-1] + last_along + last_across
    origins = [list(enumerate((a, s) for s in late)) for a in range(near)]
    origins += [list(enumerate((near * b, s) for s in early)) for b in [0, *range(far - 1, 0, -1)]]
    origins += [list(enumerate((a + near * b, s) for a in range(near) for s in late)) for b in range(far - 1, 0, -1)]
    origins += [list(enumerate((a + near * b, s) for b in range(far) for s in early)) for a in range(near - 1, 0, -1)]
    count = len(blocks)
    return pl.pallas_call(
        functools.partial(contract, origins, cap, count),
        out_shape=jax.ShapeDtypeStruct((tiles, pairs, columns), jnp.bfloat16),
        in_specs=[SMEM] * count + [VMEM] * (len(pieces) + count),
        out_specs=ANYWHERE,
        scratch_shapes=[
            pltpu.VMEM((cap * wide, pairs, columns), amplitudes.dtype),
            pltpu.VMEM((tiles, pairs, columns), jnp.bfloat16),
            pltpu.SemaphoreType.DMA((tiles,)),
        ],
        compiler_params=GRANT,
    )(*places, *pieces, *blocks)


def solution(mesh):
    placed = (
        P("wide", "narrow", None),
        P("wide", None),
        P("wide", "narrow"),
        P("wide", "narrow", None, None),
    )
    return jax.shard_map(
        functools.partial(on_device, mesh.shape["wide"], mesh.shape["narrow"]),
        mesh=mesh,
        in_specs=placed,
        out_specs=P("wide", "narrow", None),
        check_vma=False,
    )
```
